256 devices in a mesh: inst: 32 (over z_lo, y, core), tp: 8 (over x, z_hi).
Axes of the slice: x: 4, y: 4, z: 8 (z_hi: 2, z_lo: 4; z = z_hi * 4 + z_lo), core: 2. Of those that a mesh axis runs over, the one named last changes fastest.
Arguments:
- tokens_now: bfloat16 [32, 16, 4096], P('inst'), may hold values from -6 to 6
- tokens_next: bfloat16 [32, 20, 4096], P('inst'), may hold values from -6 to 6
- norm_gain: float32 [4096], replicated, may hold values from 0.1 to 1.9
- query_weight: bfloat16 [4096, 4096], P(None, 'tp'), may hold values from -0.09375 to 0.09375
- key_weight: bfloat16 [4096, 1024], P(None, 'tp'), may hold values from -0.09375 to 0.09375
- value_weight: bfloat16 [4096, 1024], P(None, 'tp'), may hold values from -0.09375 to 0.09375
- out_weight: bfloat16 [4096, 4096], P('tp'), may hold values from -0.375 to 0.375
- kv_cache: bfloat16 [32, 16, 2, 480, 1024], P('inst', None, None, None, 'tp'), may hold values from -640 to 640
- lengths: int32 [32, 16], replicated, may hold values from 2 to 478, as said below
- pairing: int32 [32], replicated, may hold values from 0 to 31, as said below
- moving: int32 [32, 4], replicated, may hold values from 0 to 15, as said below
Outputs:
- first_out: bfloat16 [32, 16, 4096], P('inst')
- second_out: bfloat16 [32, 20, 4096], P('inst')
- arrived_cache: bfloat16 [32, 4, 2, 480, 1024], P('inst', None, None, None, 'tp')
The draws below stay inside these ranges and needn't reach their ends.
Inputs may be any that keep to these rules, and one draw needn't show every extreme that they name: `lengths`: positions at and beyond a request's length hold no cached token. pairing[i] = i XOR 2^b for a bit b that may differ from pair to pair, so partners are mutual and differ in one bit. `moving`: each row names 4 different slots.
All inputs are finite; a program needn't handle non-finite values.
Results may differ from the reference program's by a relative error of at most 0.007.
The reference program's roundings to bfloat16 on the way count: a program that leaves them out, or rounds other values in their place, can miss the bound.
Values may be sent and summed in bfloat16 or wider, within the bound.
A program may use at most 256 MiB of HBM per device.

```python
import math
import jax
import jax.numpy as jnp
from jax import lax

D = 4096
HEADS = 32
KV_HEADS = 8
HD = 128
REQS = 16
SPAN = 480
MOVES = 4
INSTS = 32


def draw_kv_cache(key, part):
    key = jax.random.fold_in(key, 11)
    base_key = jax.random.fold_in(key, 0)
    shape = (INSTS, REQS, 2, SPAN, KV_HEADS * HD)
    entries = jnp.clip(jax.random.normal(base_key, shape, jnp.float32), -6.0, 6.0)
    entries = entries * jnp.array([1.5, 1.0], jnp.float32)[None, None, :, None, None]
    return entries.astype(jnp.bfloat16)


def draw_lengths(key, part):
    key = jax.random.fold_in(key, 23)
    cap_key, len_key, spot_key = jax.random.split(key, 3)
    caps = jax.random.randint(cap_key, (INSTS, 1), (SPAN - 2) // 4 + 2, SPAN - 1)
    drawn = jax.random.randint(len_key, (INSTS, REQS), 2, caps)
    spot = jax.random.randint(spot_key, (), 0, INSTS * REQS)
    flat = drawn.reshape(-1).at[spot].set(SPAN - 2)
    flat = flat.at[(spot + 1) % (INSTS * REQS)].set(2)
    return flat.reshape(INSTS, REQS).astype(jnp.int32)


def draw_pairing(key, part):
    key = jax.random.fold_in(key, 37)
    first_key, offset_key, coin_key = jax.random.split(key, 3)
    bit_count = INSTS.bit_length() - 1
    instance_ids = jnp.arange(INSTS, dtype=jnp.int32)
    if bit_count > 1:
        first_bit = jax.random.randint(first_key, (), 0, bit_count).astype(jnp.int32)
        offset_bit = jax.random.randint(offset_key, (), 1, bit_count).astype(jnp.int32)
        second_bit = ((first_bit + offset_bit) % bit_count).astype(jnp.int32)
    else:
        first_bit = jnp.int32(0)
        second_bit = jnp.int32(0)
    first_mask = jnp.left_shift(jnp.int32(1), first_bit)
    second_mask = jnp.left_shift(jnp.int32(1), second_bit)
    group_ids = jnp.bitwise_and(instance_ids, jnp.bitwise_not(jnp.bitwise_or(first_mask, second_mask)))
    coins = jax.random.randint(coin_key, (INSTS,), 0, 2).astype(jnp.int32)
    chosen = jnp.where(coins[group_ids] == 1, first_mask, second_mask)
    return jnp.bitwise_xor(instance_ids, chosen).astype(jnp.int32)


def draw_moving(key, part):
    key = jax.random.fold_in(key, 41)
    row_keys = jax.random.split(key, INSTS)
    orders = jax.vmap(lambda row_key: jax.random.permutation(row_key, REQS))(row_keys).astype(jnp.int32)
    head_row = orders[0]
    positions = jnp.arange(REQS, dtype=jnp.int32)
    head_row = jnp.where(head_row == REQS - 1, head_row[0], jnp.where(positions == 0, REQS - 1, head_row))
    head_row = jnp.where(head_row == 0, head_row[1], jnp.where(positions == 1, 0, head_row))
    orders = orders.at[0].set(head_row)
    return orders[:, :MOVES].astype(jnp.int32)


def block_levels(rng, shape, cuts, smallest, top_value):
    gain = 1.0
    for axis_at, shards_of in cuts:
        steps = jax.random.uniform(jax.random.fold_in(jax.random.fold_in(rng, 6), axis_at), (shards_of,), jnp.float32, smallest / len(cuts), top_value / len(cuts))
        gain = gain * jnp.repeat(jnp.exp(steps), shape[axis_at] // shards_of).reshape((-1,) + (1,) * (len(shape) - 1 - axis_at))
    return gain


def scatter_about(key, extent, width, reach, shards=(), kind=jnp.bfloat16):
    factor_of = block_levels(key, extent, shards, -0.22, 0.18) if shards else 1.0
    values = jax.random.normal(key, extent, jnp.float32) * width * factor_of
    return jnp.minimum(jnp.maximum(values, -reach), reach).astype(kind)


def setup_inputs(seed: int = 0) -> dict:
    streams_of = jax.random.split(jax.random.key(seed), 12)
    tokens_now = scatter_about(streams_of[0], (INSTS, REQS, D), 1.0, 6.0, ((0, 32),))
    tokens_next = scatter_about(streams_of[1], (INSTS, REQS + MOVES, D), 1.0, 6.0, ((0, 32),))
    norm_gain = jnp.clip(1.0 + 0.18 * jax.random.normal(streams_of[2], (D,), jnp.float32), 0.1, 1.9)
    query_weight = scatter_about(streams_of[3], (D, HEADS * HD), D ** -0.5, 0.09375, ((1, 8),))
    key_weight = scatter_about(streams_of[4], (D, KV_HEADS * HD), D ** -0.5, 0.09375, ((1, 8),))
    value_weight = scatter_about(streams_of[5], (D, KV_HEADS * HD), D ** -0.5, 0.09375, ((1, 8),))
    out_weight = scatter_about(streams_of[6], (HEADS * HD, D), (HEADS * HD // 16) ** -0.5, 0.375, ((0, 8),))
    kv_cache = draw_kv_cache(jax.random.fold_in(streams_of[11], 71), 0)
    lengths = draw_lengths(jax.random.fold_in(streams_of[11], 71), 0)
    pairing = draw_pairing(jax.random.fold_in(streams_of[11], 71), 0)
    moving = draw_moving(jax.random.fold_in(streams_of[11], 71), 0)
    return {"tokens_now": tokens_now, "tokens_next": tokens_next, "norm_gain": norm_gain, "query_weight": query_weight, "key_weight": key_weight, "value_weight": value_weight, "out_weight": out_weight, "kv_cache": kv_cache, "lengths": lengths, "pairing": pairing, "moving": moving}


ROPE_THETA = 500000.0
NORM_EPSILON = 1e-05

def rotate(vectors, places):
    half_dim = HD // 2
    frequency = ROPE_THETA ** (-(jnp.arange(half_dim, dtype=jnp.float32) * 2.0) / HD)
    angles = places.astype(jnp.float32)[:, None, None] * frequency
    lower_half = vectors[..., :half_dim]
    upper_half = vectors[..., half_dim:]
    cosine = jnp.cos(angles)
    sine_part = jnp.sin(angles)
    return jnp.concatenate([lower_half * cosine - upper_half * sine_part, upper_half * cosine + lower_half * sine_part], axis=-1)

def project(token_rows, places, norm_gain, query_weight, key_weight, value_weight):
    widened = token_rows.astype(jnp.float32)
    row_scale = lax.rsqrt(lax.optimization_barrier(jnp.mean(widened * widened, axis=-1, keepdims=True)) + NORM_EPSILON)
    normed = (widened * row_scale * norm_gain).astype(jnp.bfloat16)
    row_count = token_rows.shape[0]
    query = jnp.dot(normed, query_weight, preferred_element_type=jnp.float32).reshape(row_count, -1, HD)
    new_key = jnp.dot(normed, key_weight, preferred_element_type=jnp.float32).reshape(row_count, -1, HD)
    new_value = jnp.dot(normed, value_weight, preferred_element_type=jnp.float32).astype(jnp.bfloat16)
    query = rotate(query, places).astype(jnp.bfloat16)
    new_key = rotate(new_key, places).astype(jnp.bfloat16).reshape(row_count, -1)
    return (query, new_key, new_value)

def attend(query, stored_keys, stored_values, visible, fresh_key, fresh_value):
    row_count = query.shape[0]
    group_size = HEADS // KV_HEADS
    grouped = query.astype(jnp.float32).reshape(row_count, KV_HEADS, group_size, HD)
    all_keys = jnp.concatenate([stored_keys, fresh_key[:, None, :]], axis=1).astype(jnp.float32).reshape(row_count, -1, KV_HEADS, HD)
    all_values = jnp.concatenate([stored_values, fresh_value[:, None, :]], axis=1).astype(jnp.float32).reshape(row_count, -1, KV_HEADS, HD)
    seen = jnp.concatenate([visible, jnp.ones_like(visible[:, :1])], axis=1)
    scores = jnp.einsum('nkgd,nskd->nkgs', grouped, all_keys) * (1.0 / math.sqrt(HD))
    scores = jnp.where(seen[:, None, None, :], scores, -jnp.inf)
    largest = lax.optimization_barrier(jnp.max(scores, axis=-1, keepdims=True))
    raised = jnp.exp(scores - largest)
    weights = (raised / lax.optimization_barrier(jnp.sum(raised, axis=-1, keepdims=True))).astype(jnp.bfloat16)
    mixed = jnp.einsum('nkgs,nskd->nkgd', weights.astype(jnp.float32), all_values)
    return mixed.astype(jnp.bfloat16).reshape(row_count, HEADS * HD)

def attend_member(member):
    return attend(member[0], member[1], member[2], member[3], member[4], member[5])

def reference(tokens_now, tokens_next, norm_gain, query_weight, key_weight, value_weight, out_weight, kv_cache, lengths, pairing, moving):
    instance_ids = jnp.arange(INSTS, dtype=jnp.int32)
    loads = lax.optimization_barrier(jnp.sum(lengths, axis=1))
    partner = pairing
    sender = (loads > loads[partner]) | (loads == loads[partner]) & (instance_ids < partner)
    receiver = jnp.logical_not(sender)
    places = jnp.arange(SPAN, dtype=jnp.int32)
    query_one, key_one, value_one = project(tokens_now.reshape(-1, D), lengths.reshape(-1), norm_gain, query_weight, key_weight, value_weight)
    query_one = query_one.reshape(INSTS, REQS, HEADS, HD)
    key_one = key_one.reshape(INSTS, REQS, -1)
    value_one = value_one.reshape(INSTS, REQS, -1)
    stored_keys = kv_cache[:, :, 0]
    stored_values = kv_cache[:, :, 1]
    visible_one = places[None, None, :] < lengths[:, :, None]
    attended_one = lax.map(attend_member, (query_one, stored_keys, stored_values, visible_one, key_one, value_one))
    first_out = jnp.dot(attended_one.reshape(-1, HEADS * HD), out_weight, preferred_element_type=jnp.float32).astype(jnp.bfloat16).reshape(INSTS, REQS, D)
    at_len = (places[None, None, :] == lengths[:, :, None])[..., None]
    extended_keys = jnp.where(at_len, key_one[:, :, None, :], stored_keys)
    extended_values = jnp.where(at_len, value_one[:, :, None, :], stored_values)
    in_slots = moving[partner]
    in_len = lengths[partner[:, None], in_slots]
    keep = (places[None, None, :] <= in_len[:, :, None]) & receiver[:, None, None]
    arrived_keys = jnp.where(keep[..., None], extended_keys[partner[:, None], in_slots], jnp.zeros((), jnp.bfloat16))
    arrived_values = jnp.where(keep[..., None], extended_values[partner[:, None], in_slots], jnp.zeros((), jnp.bfloat16))
    arrived_cache = jnp.stack([arrived_keys, arrived_values], axis=2)
    step_len = jnp.concatenate([lengths, in_len], axis=1)
    query_two, key_two, value_two = project(tokens_next.reshape(-1, D), (step_len + 1).reshape(-1), norm_gain, query_weight, key_weight, value_weight)
    query_two = query_two.reshape(INSTS, REQS + MOVES, HEADS, HD)
    key_two = key_two.reshape(INSTS, REQS + MOVES, -1)
    value_two = value_two.reshape(INSTS, REQS + MOVES, -1)
    keys_two = jnp.concatenate([extended_keys, arrived_keys], axis=1)
    values_two = jnp.concatenate([extended_values, arrived_values], axis=1)
    visible_two = places[None, None, :] <= step_len[:, :, None]
    attended_two = lax.map(attend_member, (query_two, keys_two, values_two, visible_two, key_two, value_two))
    second = jnp.dot(attended_two.reshape(-1, HEADS * HD), out_weight, preferred_element_type=jnp.float32).astype(jnp.bfloat16).reshape(INSTS, REQS + MOVES, D)
    departed = jnp.any(jnp.arange(REQS, dtype=jnp.int32)[None, :, None] == moving[:, None, :], axis=2) & sender[:, None]
    live = jnp.concatenate([jnp.logical_not(departed), jnp.broadcast_to(receiver[:, None], (INSTS, MOVES))], axis=1)
    second_out = jnp.where(live[:, :, None], second, jnp.zeros((), jnp.bfloat16))
    return (first_out, second_out, arrived_cache)
```

```python
import functools
import math

import jax
import jax.numpy as jnp
import numpy as np
from jax import lax
from jax.experimental import pallas as pl
from jax.experimental.pallas import tpu as pltpu
from jax.sharding import PartitionSpec as P

HD = 128
ROPE_THETA = 500000.0
NORM_EPSILON = 1e-05
MESH = pl.DeviceIdType.MESH
F32 = jnp.float32
BF16 = jnp.bfloat16
LIMIT = 40 * 1024 * 1024

ROWS = 48
REQS = 16
MOVES = 4
SPAN = 480
TILE = 16
PARCEL = 2 * MOVES * SPAN
SIZES = 8
STRIDE = PARCEL // SIZES


def role(lengths, pairing):
    me = lax.axis_index("inst")
    partner = pairing[me]
    mine = lengths[me, 0]
    theirs = lengths[partner, 0]
    for slot in range(1, REQS):
        mine = mine + lengths[me, slot]
        theirs = theirs + lengths[partner, slot]
    sender = (mine > theirs) | ((mine == theirs) & (me < partner))
    return me, partner, sender


def put_row(cache, lead, place, row):
    base = pl.multiple_of((place // TILE) * TILE, TILE)
    at = lead + (pl.ds(base, TILE), slice(None))
    held = cache[at].astype(F32)
    here = lax.broadcasted_iota(jnp.int32, (TILE, HD), 0) == place - base
    cache[at] = jnp.where(here, jnp.broadcast_to(row, (TILE, HD)), held).astype(BF16)


def front_kernel(
    lengths,
    pairing,
    moving,
    frequency,
    tokens_now,
    tokens_next,
    norm_gain,
    key_weight,
    value_weight,
    kv_cache,
    normed_out,
    turn_out,
    new_key,
    new_value,
    parcel_out,
    choice_out,
    key_held,
    value_held,
    parcel,
    weight_sem,
    cache_sem,
    out_sem,
):
    me, partner, sender = role(lengths, pairing)
    weight_copies = []
    for index, (source, held) in enumerate(((key_weight, key_held), (value_weight, value_held))):
        copy = pltpu.make_async_copy(source, held, weight_sem.at[index])
        copy.start()
        weight_copies.append(copy)
    offset = 0
    cache_copies = []
    places = []
    for move in range(MOVES):
        slot = moving[me, move]
        length = lengths[me, slot]
        size = pl.multiple_of((length // TILE + 1) * TILE, TILE)
        for kind in range(2):
            start = pl.multiple_of(offset + kind * size, TILE)
            copy = pltpu.make_async_copy(
                kv_cache.at[slot, kind, pl.ds(0, size)],
                parcel.at[pl.ds(start, size)],
                cache_sem.at[2 * move + kind],
            )
            copy.start()
            cache_copies.append(copy)
            places.append((slot, start + length))
        offset = offset + 2 * size
    total = 0
    giver = jnp.where(sender, me, partner)
    for move in range(MOVES):
        total = total + (lengths[giver, moving[giver, move]] // TILE + 1) * (2 * TILE)
    distance = me ^ partner
    bit = (
        (distance >= 2).astype(jnp.int32)
        + (distance >= 4).astype(jnp.int32)
        + (distance >= 8).astype(jnp.int32)
        + (distance >= 16).astype(jnp.int32)
    )
    upward = (sender == (me < partner)).astype(jnp.int32)
    size_class = (total + STRIDE - 1) // STRIDE - 1
    choice_out[0] = (bit * 2 + upward) * SIZES + size_class

    row_at = lax.broadcasted_iota(jnp.int32, (ROWS, HD), 0)
    times = jnp.zeros((ROWS, HD), jnp.int32)
    for slot in range(REQS):
        times = jnp.where(row_at == slot, lengths[me, slot], times)
        times = jnp.where(row_at == REQS + slot, lengths[me, slot] + 1, times)
    for move in range(MOVES):
        in_length = lengths[partner, moving[partner, move]]
        times = jnp.where(row_at == 2 * REQS + move, in_length + 1, times)
    angles = times.astype(F32) * frequency[...]
    lane_at = lax.broadcasted_iota(jnp.int32, (ROWS, HD), 1)
    cosine = jnp.cos(angles)
    sine = jnp.sin(angles)
    sine = jnp.where(lane_at < HD // 2, -sine, sine)
    turn_out[0] = cosine
    turn_out[1] = sine

    gain = norm_gain[...]
    normed_out[2 * REQS :, :] = jnp.zeros((ROWS - 2 * REQS, normed_out.shape[1]), BF16)
    for rows, base in ((tokens_now, 0), (tokens_next, REQS)):
        count = rows.shape[0]
        widened = rows[...].astype(F32)
        scale = lax.rsqrt(jnp.mean(widened * widened, axis=-1, keepdims=True) + NORM_EPSILON)
        normed_out[base : base + count, :] = (widened * scale * gain).astype(BF16)

    for copy in weight_copies:
        copy.wait()
    normed = normed_out[...]
    key = jnp.dot(normed, key_held[...], preferred_element_type=F32)
    value = jnp.dot(normed, value_held[...], preferred_element_type=F32)
    key = key * cosine + pltpu.roll(key, HD // 2, 1) * sine
    new_key[...] = key.astype(BF16).astype(F32)
    new_value[...] = value.astype(BF16).astype(F32)

    for copy in cache_copies:
        copy.wait()
    for index, (slot, place) in enumerate(places):
        fresh = (new_key, new_value)[index % 2]
        put_row(parcel, (), place, fresh[pl.ds(slot, 1), :])
    out_copy = pltpu.make_async_copy(parcel, parcel_out, out_sem)
    out_copy.start()
    out_copy.wait()


def softmax_rows(scores):
    largest = jnp.max(scores, axis=-1, keepdims=True)
    raised = jnp.exp(scores - largest)
    return raised / jnp.sum(raised, axis=-1, keepdims=True)


def score_block(query, keys, limit):
    scores = lax.dot_general(
        query.astype(BF16), keys, (((1,), (1,)), ((), ())), preferred_element_type=F32
    ) * (1.0 / math.sqrt(HD))
    lane_at = lax.broadcasted_iota(jnp.int32, scores.shape, 1)
    return jnp.where(lane_at <= limit, scores, -jnp.inf)


def own_kernel(
    lengths,
    normed,
    turn,
    new_key,
    new_value,
    query_weight,
    kv_cache,
    attended,
    in_query,
    weight_held,
    cache,
    query,
    scores,
    weight_sem,
    cache_sem,
):
    me = lax.axis_index("inst")
    depth = weight_held.shape[1]
    weight_copies = []
    for part in range(weight_held.shape[0]):
        copy = pltpu.make_async_copy(
            query_weight.at[pl.ds(part * depth, depth)], weight_held.at[part], weight_sem.at[part]
        )
        copy.start()
        weight_copies.append(copy)
    cache_copies = []
    for slot in range(REQS):
        copy = pltpu.make_async_copy(kv_cache.at[slot], cache.at[slot], cache_sem.at[slot])
        copy.start()
        cache_copies.append(copy)
    total = jnp.zeros((ROWS, weight_held.shape[2]), F32)
    for part, copy in enumerate(weight_copies):
        copy.wait()
        total = total + jnp.dot(
            normed[:, part * depth : (part + 1) * depth],
            weight_held[part],
            preferred_element_type=F32,
        )
    in_query[...] = jnp.zeros(in_query.shape, F32)
    for head in range(4):
        part = total[:, head * HD : (head + 1) * HD]
        part = part * turn[0] + pltpu.roll(part, HD // 2, 1) * turn[1]
        part = part.astype(BF16).astype(F32)
        for slot in range(REQS):
            query[8 * slot + head : 8 * slot + head + 1, :] = part[slot : slot + 1]
            query[8 * slot + 4 + head : 8 * slot + 5 + head, :] = part[REQS + slot : REQS + slot + 1]
        for move in range(MOVES):
            in_query[8 * move + head : 8 * move + head + 1, :] = part[
                2 * REQS + move : 2 * REQS + move + 1
            ]
    row_at = lax.broadcasted_iota(jnp.int32, (8, SPAN), 0)
    late = (row_at >= 4).astype(jnp.int32)
    for slot in range(REQS):
        cache_copies[slot].wait()
        length = lengths[me, slot]
        for kind, fresh in ((0, new_key), (1, new_value)):
            put_row(cache, (slot, kind), length, fresh[slot : slot + 1, :])
            put_row(cache, (slot, kind), length + 1, fresh[REQS + slot : REQS + slot + 1, :])
        scores[8 * slot : 8 * slot + 8, :] = score_block(
            query[8 * slot : 8 * slot + 8, :], cache[slot, 0], length + late
        )
    scores[...] = softmax_rows(scores[...])
    attended[2 * REQS :, :] = jnp.zeros((ROWS - 2 * REQS, attended.shape[1]), F32)
    for slot in range(REQS):
        mixed = jnp.dot(
            scores[8 * slot : 8 * slot + 8, :].astype(BF16),
            cache[slot, 1],
            preferred_element_type=F32,
        )
        for head in range(4):
            columns = slice(head * HD, (head + 1) * HD)
            attended[slot : slot + 1, columns] = mixed[head : head + 1]
            attended[REQS + slot : REQS + slot + 1, columns] = mixed[4 + head : 5 + head]


def incoming_kernel(
    lengths,
    pairing,
    moving,
    new_key,
    new_value,
    in_query,
    own_attended,
    parcel,
    arrived,
    attended,
    cache,
    scores,
    joined,
    in_sem,
    out_sem,
):
    me, partner, sender = role(lengths, pairing)
    receiver = jnp.logical_not(sender)
    joined[...] = own_attended[...]
    cache[...] = jnp.zeros(cache.shape, BF16)
    in_lengths = [lengths[partner, moving[partner, move]] for move in range(MOVES)]

    @pl.when(receiver)
    def _():
        offset = 0
        copies = []
        for move in range(MOVES):
            size = pl.multiple_of((in_lengths[move] // TILE + 1) * TILE, TILE)
            for kind in range(2):
                start = pl.multiple_of(offset + kind * size, TILE)
                copy = pltpu.make_async_copy(
                    parcel.at[pl.ds(start, size)],
                    cache.at[move, kind, pl.ds(0, size)],
                    in_sem.at[2 * move + kind],
                )
                copy.start()
                copies.append(copy)
            offset = offset + 2 * size
        for copy in copies:
            copy.wait()
        for move in range(MOVES):
            base = pl.multiple_of((in_lengths[move] // TILE) * TILE, TILE)
            here = lax.broadcasted_iota(jnp.int32, (TILE, HD), 0) <= in_lengths[move] - base
            for kind in range(2):
                at = (move, kind, pl.ds(base, TILE), slice(None))
                cache[at] = jnp.where(here, cache[at].astype(F32), 0.0).astype(BF16)

    out_copy = pltpu.make_async_copy(cache, arrived, out_sem)
    out_copy.start()
    out_copy.wait()
    for move in range(MOVES):
        row = 2 * REQS + move
        for kind, fresh in ((0, new_key), (1, new_value)):
            put_row(cache, (move, kind), in_lengths[move] + 1, fresh[row : row + 1, :])
        scores[8 * move : 8 * move + 8, :] = score_block(
            in_query[8 * move : 8 * move + 8, :], cache[move, 0], in_lengths[move] + 1
        )
    scores[...] = softmax_rows(scores[...])
    for move in range(MOVES):
        mixed = jnp.dot(
            scores[8 * move : 8 * move + 8, :].astype(BF16),
            cache[move, 1],
            preferred_element_type=F32,
        )
        row = 2 * REQS + move
        for head in range(4):
            joined[row : row + 1, head * HD : (head + 1) * HD] = mixed[head : head + 1]
    row_at = lax.broadcasted_iota(jnp.int32, joined.shape, 0)
    gone = row_at >= 2 * REQS
    for move in range(MOVES):
        gone = gone | (row_at == REQS + moving[me, move])
    dead = gone & (jnp.broadcast_to(sender.astype(jnp.int32), joined.shape) == 1)
    attended[...] = jnp.where(dead, 0.0, joined[...]).astype(BF16)


def fold(block):
    pieces = [block[32:36, 256 * part : 256 * (part + 1)] for part in range(4)]
    return block[:REQS], jnp.concatenate([block[REQS : 2 * REQS], jnp.concatenate(pieces, axis=0)], axis=1)


def out_kernel(
    attended,
    out_weight,
    first_out,
    second_out,
    weight_held,
    part_a,
    part_b,
    from_x_a,
    from_x_b,
    sum_a,
    sum_b,
    from_z_a,
    from_z_b,
    whole_a,
    whole_b,
    weight_sem,
    x_send,
    x_recv,
    z_send,
    z_recv,
    g_send,
    g_recv,
):
    me = lax.axis_index("inst")
    lane = lax.axis_index("tp")
    x = lane // 2
    z = lane % 2
    x_peers = [(me, lax.rem(x + step, 4) * 2 + z) for step in range(1, 4)]
    z_peer = (me, x * 2 + 1 - z)
    barrier = pltpu.get_barrier_semaphore()
    for peer in x_peers + [z_peer]:
        pl.semaphore_signal(barrier, inc=1, device_id=peer, device_id_type=MESH)
    width = weight_held.shape[2]
    order = (2, 1, 3, 0)
    weight_copies = {}
    for step in order:
        begin = pl.multiple_of(lax.rem(x + step, 4) * width, width)
        copy = pltpu.make_async_copy(
            out_weight.at[:, pl.ds(begin, width)], weight_held.at[step], weight_sem.at[step]
        )
        copy.start()
        weight_copies[step] = copy
    rows = attended[...]
    pl.semaphore_wait(barrier, 4)
    parts = (part_a, part_b)
    landed = (from_x_a, from_x_b)
    sums = (sum_a, sum_b)
    other = (from_z_a, from_z_b)
    whole = (whole_a, whole_b)
    x_copies = {}
    for step in order:
        weight_copies[step].wait()
        block = jnp.dot(rows, weight_held[step], preferred_element_type=F32)
        for half, value in enumerate(fold(block)):
            parts[half][step] = value
            if step:
                copy = pltpu.make_async_remote_copy(
                    src_ref=parts[half].at[step],
                    dst_ref=landed[half].at[step - 1],
                    send_sem=x_send.at[half, step - 1],
                    recv_sem=x_recv.at[half, step - 1],
                    device_id=x_peers[step - 1],
                    device_id_type=MESH,
                )
                copy.start()
                x_copies[half, step] = copy
    z_copies = []
    for half in range(2):
        for step in range(1, 4):
            x_copies[half, step].wait_recv()
        sums[half][...] = (parts[half][0] + landed[half][0]) + (landed[half][1] + landed[half][2])
        copy = pltpu.make_async_remote_copy(
            src_ref=sums[half],
            dst_ref=other[half],
            send_sem=z_send.at[half],
            recv_sem=z_recv.at[half],
            device_id=z_peer,
            device_id_type=MESH,
        )
        copy.start()
        z_copies.append(copy)
    g_copies = []
    for half in range(2):
        z_copies[half].wait_recv()
        whole[half][x] = (sums[half][...] + other[half][...]).astype(BF16)
        for step in range(1, 4):
            copy = pltpu.make_async_remote_copy(
                src_ref=whole[half].at[x],
                dst_ref=whole[half].at[x],
                send_sem=g_send.at[half, step - 1],
                recv_sem=g_recv.at[half, step - 1],
                device_id=x_peers[step - 1],
                device_id_type=MESH,
            )
            copy.start()
            g_copies.append(copy)
    for copy in g_copies:
        copy.wait_recv()
    for chunk in range(4):
        columns = slice(chunk * width, (chunk + 1) * width)
        first_out[:, columns] = whole_a[chunk]
        block = whole_b[chunk]
        second_out[:REQS, columns] = block[:, :width]
        folded = block[:, width:].astype(F32)
        pieces = [folded[4 * part : 4 * part + 4] for part in range(4)]
        second_out[REQS:, columns] = jnp.concatenate(pieces, axis=1).astype(BF16)
    for copy in list(x_copies.values()) + z_copies + g_copies:
        copy.wait_send()


def route(bit, upward):
    pairs = []
    for low in range(32):
        high = low | 1 << bit
        if high != low:
            pairs.append((low, high) if upward else (high, low))
    return pairs


def send_branch(bit, upward, size, parcel):
    moved = lax.ppermute(parcel[: size * STRIDE], "inst", route(bit, upward))
    return lax.dynamic_update_slice(parcel, moved, (0, 0))


def body(
    tokens_now,
    tokens_next,
    norm_gain,
    query_weight,
    key_weight,
    value_weight,
    out_weight,
    kv_cache,
    lengths,
    pairing,
    moving,
):
    smem = pl.BlockSpec(memory_space=pltpu.SMEM)
    vmem = pl.BlockSpec(memory_space=pltpu.VMEM)
    hbm = pl.BlockSpec(memory_space=pl.ANY)
    params = pltpu.CompilerParams(vmem_limit_bytes=LIMIT)
    d = tokens_now.shape[-1]
    wide = query_weight.shape[1]
    stored = kv_cache[0]
    half = ROPE_THETA ** (-(np.arange(HD // 2, dtype=np.float32) * 2.0) / HD)
    frequency = np.concatenate([half, half]).astype(np.float32)[None, :]
    shape = jax.ShapeDtypeStruct
    normed, turn, new_key, new_value, parcel, choice = pl.pallas_call(
        front_kernel,
        out_shape=(
            shape((ROWS, d), BF16),
            shape((2, ROWS, HD), F32),
            shape((ROWS, HD), F32),
            shape((ROWS, HD), F32),
            shape((PARCEL, HD), BF16),
            shape((1,), jnp.int32),
        ),
        in_specs=[smem] * 3 + [vmem] * 4 + [hbm] * 3,
        out_specs=(vmem, vmem, vmem, vmem, hbm, smem),
        scratch_shapes=[
            pltpu.VMEM((d, HD), BF16),
            pltpu.VMEM((d, HD), BF16),
            pltpu.VMEM((PARCEL, HD), BF16),
            pltpu.SemaphoreType.DMA((2,)),
            pltpu.SemaphoreType.DMA((2 * MOVES,)),
            pltpu.SemaphoreType.DMA,
        ],
        compiler_params=params,
        name="front",
    )(
        lengths,
        pairing,
        moving,
        frequency,
        tokens_now[0],
        tokens_next[0],
        norm_gain[None, :],
        key_weight,
        value_weight,
        stored,
    )
    branches = [
        functools.partial(send_branch, bit, upward, size)
        for bit in range(5)
        for upward in (0, 1)
        for size in range(1, SIZES + 1)
    ]
    moved = lax.switch(choice[0], branches, parcel)
    own_attended, in_query = pl.pallas_call(
        own_kernel,
        out_shape=(shape((ROWS, wide), F32), shape((8 * MOVES, HD), F32)),
        in_specs=[smem] + [vmem] * 4 + [hbm] * 2,
        out_specs=(vmem, vmem),
        scratch_shapes=[
            pltpu.VMEM((4, d // 4, wide), BF16),
            pltpu.VMEM(stored.shape, BF16),
            pltpu.VMEM((8 * REQS, HD), F32),
            pltpu.VMEM((8 * REQS, SPAN), F32),
            pltpu.SemaphoreType.DMA((4,)),
            pltpu.SemaphoreType.DMA((REQS,)),
        ],
        compiler_params=params,
        name="own",
    )(lengths, normed, turn, new_key, new_value, query_weight, stored)
    arrived, attended = pl.pallas_call(
        incoming_kernel,
        out_shape=(shape((MOVES, 2, SPAN, HD), BF16), shape((ROWS, wide), BF16)),
        in_specs=[smem] * 3 + [vmem] * 4 + [hbm],
        out_specs=(hbm, vmem),
        scratch_shapes=[
            pltpu.VMEM((MOVES, 2, SPAN, HD), BF16),
            pltpu.VMEM((8 * MOVES, SPAN), F32),
            pltpu.VMEM((ROWS, wide), F32),
            pltpu.SemaphoreType.DMA((2 * MOVES,)),
            pltpu.SemaphoreType.DMA,
        ],
        compiler_params=params,
        name="incoming",
    )(lengths, pairing, moving, new_key, new_value, in_query, own_attended, moved)
    width = d // 4
    side = width + MOVES * width // REQS
    first, second = pl.pallas_call(
        out_kernel,
        out_shape=(shape((REQS, d), BF16), shape((REQS + MOVES, d), BF16)),
        in_specs=[vmem, hbm],
        out_specs=(vmem, vmem),
        scratch_shapes=[
            pltpu.VMEM((4, wide, width), BF16),
            pltpu.VMEM((4, REQS, width), F32),
            pltpu.VMEM((4, REQS, side), F32),
            pltpu.VMEM((3, REQS, width), F32),
            pltpu.VMEM((3, REQS, side), F32),
            pltpu.VMEM((REQS, width), F32),
            pltpu.VMEM((REQS, side), F32),
            pltpu.VMEM((REQS, width), F32),
            pltpu.VMEM((REQS, side), F32),
            pltpu.VMEM((4, REQS, width), BF16),
            pltpu.VMEM((4, REQS, side), BF16),
            pltpu.SemaphoreType.DMA((4,)),
            pltpu.SemaphoreType.DMA((2, 3)),
            pltpu.SemaphoreType.DMA((2, 3)),
            pltpu.SemaphoreType.DMA((2,)),
            pltpu.SemaphoreType.DMA((2,)),
            pltpu.SemaphoreType.DMA((2, 3)),
            pltpu.SemaphoreType.DMA((2, 3)),
        ],
        compiler_params=pltpu.CompilerParams(
            vmem_limit_bytes=LIMIT, collective_id=0, has_side_effects=True
        ),
        name="project_out",
    )(attended, out_weight)
    return first[None], second[None], arrived[None]


def solution(mesh):
    in_specs = (
        P("inst", None, None),
        P("inst", None, None),
        P(),
        P(None, "tp"),
        P(None, "tp"),
        P(None, "tp"),
        P("tp", None),
        P("inst", None, None, None, "tp"),
        P(),
        P(),
        P(),
    )
    out_specs = (P("inst", None, None), P("inst", None, None), P("inst", None, None, None, "tp"))
    return jax.shard_map(body, mesh=mesh, in_specs=in_specs, out_specs=out_specs, check_vma=False)
```

```python
import functools
import math

import jax
import jax.numpy as jnp
import numpy as np
from jax import lax
from jax.experimental import pallas as pl
from jax.experimental.pallas import tpu as pltpu
from jax.sharding import PartitionSpec as P

HD = 128
ROPE_THETA = 500000.0
NORM_EPSILON = 1e-05
MESH = pl.DeviceIdType.MESH
F32 = jnp.float32
BF16 = jnp.bfloat16
LIMIT = 60 * 1024 * 1024

ROWS = 48
REQS = 16
MOVES = 4
SPAN = 480
TILE = 16
PARCEL = 2 * MOVES * SPAN
SIZES = 8
STRIDE = PARCEL // SIZES
SPLITS = (1024, 2304)


def role(lengths, pairing):
    me = lax.axis_index("inst")
    partner = pairing[me]
    mine = lengths[0, me]
    theirs = lengths[0, partner]
    for slot in range(1, REQS):
        mine = mine + lengths[slot, me]
        theirs = theirs + lengths[slot, partner]
    sender = (mine > theirs) | ((mine == theirs) & (me < partner))
    return me, partner, sender


def load(copies):
    started = []
    for source, target, semaphore in copies:
        copy = pltpu.make_async_copy(source, target, semaphore)
        copy.start()
        started.append(copy)
    return started


def softmax_rows(scores):
    largest = jnp.max(scores, axis=-1, keepdims=True)
    raised = jnp.exp(scores - largest)
    return raised / jnp.sum(raised, axis=-1, keepdims=True)


def score_block(query, keys, limit):
    scores = lax.dot_general(
        query.astype(BF16), keys, (((1,), (1,)), ((), ())), preferred_element_type=F32
    ) * (1.0 / math.sqrt(HD))
    lane_at = lax.broadcasted_iota(jnp.int32, scores.shape, 1)
    return jnp.where(lane_at <= limit, scores, -jnp.inf)


def front_kernel(
    lengths_hbm,
    pairing_hbm,
    moving_hbm,
    frequency_hbm,
    tokens_now_hbm,
    tokens_next_hbm,
    norm_gain_hbm,
    key_weight,
    value_weight,
    query_weight,
    kv_cache,
    parcel_hbm,
    carry_hbm,
    way_out,
    size_out,
    lengths,
    pairing,
    moving,
    frequency,
    tokens_now,
    tokens_next,
    norm_gain,
    key_held,
    value_held,
    query_held,
    cache,
    normed,
    new_key,
    new_value,
    query,
    scores,
    carry,
    fact_sem,
    token_sem,
    weight_sem,
    query_sem,
    cache_sem,
    parcel_sem,
    carry_sem,
):
    facts = load(
        [
            (lengths_hbm, lengths, fact_sem.at[0]),
            (pairing_hbm, pairing, fact_sem.at[1]),
            (moving_hbm, moving, fact_sem.at[2]),
            (frequency_hbm, frequency, fact_sem.at[3]),
        ]
    )
    tokens = load(
        [
            (tokens_now_hbm, tokens_now, token_sem.at[0]),
            (tokens_next_hbm, tokens_next, token_sem.at[1]),
            (norm_gain_hbm, norm_gain, token_sem.at[2]),
        ]
    )
    weights = load(
        [
            (key_weight, key_held, weight_sem.at[0]),
            (value_weight, value_held, weight_sem.at[1]),
        ]
    )
    for slot in range(REQS):
        cache[slot, 1] = jnp.zeros((SPAN, HD), BF16)
    for copy in facts:
        copy.wait()
    me, partner, sender = role(lengths, pairing)
    caches = []
    for slot in range(REQS):
        size = pl.multiple_of(((lengths[slot, me] + 1) // TILE + 1) * TILE, TILE)
        caches.append(
            (
                kv_cache.at[slot, :, pl.ds(0, size)],
                cache.at[slot, :, pl.ds(0, size)],
                cache_sem.at[slot],
            )
        )
    caches = load(caches)
    depth = query_held.shape[0] // 4
    queries = load(
        [
            (
                query_weight.at[pl.ds(depth * part, depth)],
                query_held.at[pl.ds(depth * part, depth)],
                query_sem.at[part],
            )
            for part in range(4)
        ]
    )
    total = 0
    giver = jnp.where(sender, me, partner)
    for move in range(MOVES):
        total = total + (lengths[moving[move, giver], giver] // TILE + 1) * (2 * TILE)
    distance = me ^ partner
    bit = (
        (distance >= 2).astype(jnp.int32)
        + (distance >= 4).astype(jnp.int32)
        + (distance >= 8).astype(jnp.int32)
        + (distance >= 16).astype(jnp.int32)
    )
    upward = (sender == (me < partner)).astype(jnp.int32)
    way_out[0] = bit * 2 + upward
    size_out[0] = (total + STRIDE - 1) // STRIDE - 1

    row_at = lax.broadcasted_iota(jnp.int32, (ROWS, HD), 0)
    times = jnp.zeros((ROWS, HD), jnp.int32)
    for slot in range(REQS):
        times = jnp.where(row_at == slot, lengths[slot, me], times)
        times = jnp.where(row_at == REQS + slot, lengths[slot, me] + 1, times)
    for move in range(MOVES):
        in_length = lengths[moving[move, partner], partner]
        times = jnp.where(row_at == 2 * REQS + move, in_length + 1, times)
    angles = times.astype(F32) * frequency[...]
    lane_at = lax.broadcasted_iota(jnp.int32, (ROWS, HD), 1)
    cosine = jnp.cos(angles)
    sine = jnp.sin(angles)
    sine = jnp.where(lane_at < HD // 2, -sine, sine)

    for copy in tokens:
        copy.wait()
    gain = norm_gain[...]
    normed[2 * REQS :, :] = jnp.zeros((ROWS - 2 * REQS, normed.shape[1]), BF16)
    for rows, base in ((tokens_now, 0), (tokens_next, REQS)):
        count = rows.shape[0]
        widened = rows[...].astype(F32)
        scale = lax.rsqrt(jnp.mean(widened * widened, axis=-1, keepdims=True) + NORM_EPSILON)
        normed[base : base + count, :] = (widened * scale * gain).astype(BF16)

    for copy in weights:
        copy.wait()
    key = jnp.dot(normed[...], key_held[...], preferred_element_type=F32)
    value = jnp.dot(normed[...], value_held[...], preferred_element_type=F32)
    key = key * cosine + pltpu.roll(key, HD // 2, 1) * sine
    new_key[...] = key.astype(BF16).astype(F32)
    new_value[...] = value.astype(BF16).astype(F32)

    for slot in range(REQS):
        caches[slot].wait()
    window_at = lax.broadcasted_iota(jnp.int32, (2 * TILE, HD), 0)
    for group in range(0, REQS, 4):
        changed = []
        for slot in range(group, group + 4):
            length = lengths[slot, me]
            base = pl.multiple_of(jnp.minimum(length // TILE * TILE, SPAN - 2 * TILE), TILE)
            for kind, fresh in ((0, new_key), (1, new_value)):
                at = (slot, kind, pl.ds(base, 2 * TILE), slice(None))
                held = cache[at].astype(F32)
                for row, place in ((slot, length), (REQS + slot, length + 1)):
                    held = jnp.where(
                        window_at == place - base,
                        jnp.broadcast_to(fresh[row : row + 1, :], held.shape),
                        held,
                    )
                changed.append((at, held.astype(BF16)))
        for at, held in changed:
            cache[at] = held
    offset = 0
    parcels = []
    for move in range(MOVES):
        slot = moving[move, me]
        size = pl.multiple_of((lengths[slot, me] // TILE + 1) * TILE, TILE)
        for kind in range(2):
            start = pl.multiple_of(offset + kind * size, TILE)
            parcels.append(
                (
                    cache.at[slot, kind, pl.ds(0, size)],
                    parcel_hbm.at[pl.ds(start, size)],
                    parcel_sem.at[2 * move + kind],
                )
            )
        offset = offset + 2 * size
    parcels = load(parcels)

    wide = query_held.shape[1]
    total = jnp.zeros((ROWS, wide), F32)
    for part in range(4):
        queries[part].wait()
        columns = slice(depth * part, depth * (part + 1))
        total = total + jnp.dot(
            normed[:, columns], query_held[columns, :], preferred_element_type=F32
        )
    carry[...] = jnp.zeros(carry.shape, F32)
    for head in range(4):
        columns = slice(head * HD, (head + 1) * HD)
        part = total[:, columns]
        part = part * cosine + pltpu.roll(part, HD // 2, 1) * sine
        part = part.astype(BF16).astype(F32)
        for slot in range(REQS):
            query[8 * slot + head : 8 * slot + head + 1, :] = part[slot : slot + 1]
            query[8 * slot + 4 + head : 8 * slot + 5 + head, :] = part[REQS + slot : REQS + slot + 1]
        carry[ROWS : ROWS + MOVES, columns] = part[2 * REQS : 2 * REQS + MOVES]
    carry[ROWS + 8 : ROWS + 8 + MOVES, :HD] = new_key[2 * REQS : 2 * REQS + MOVES, :]
    carry[ROWS + 8 : ROWS + 8 + MOVES, HD : 2 * HD] = new_value[2 * REQS : 2 * REQS + MOVES, :]
    carry[ROWS + 8 : ROWS + 8 + MOVES, 2 * HD : 3 * HD] = times[2 * REQS : 2 * REQS + MOVES].astype(F32)
    carry[ROWS + 8 : ROWS + 8 + MOVES, 3 * HD :] = jnp.broadcast_to(
        jnp.logical_not(sender).astype(F32), (MOVES, HD)
    )
    late = (lax.broadcasted_iota(jnp.int32, (8, SPAN), 0) >= 4).astype(jnp.int32)
    for slot in range(REQS):
        scores[8 * slot : 8 * slot + 8, :] = score_block(
            query[8 * slot : 8 * slot + 8, :], cache[slot, 0], lengths[slot, me] + late
        )
    for group in range(4):
        rows = slice(32 * group, 32 * group + 32)
        scores[rows, :] = softmax_rows(scores[rows, :])
    for slot in range(REQS):
        mixed = jnp.dot(
            scores[8 * slot : 8 * slot + 8, :].astype(BF16),
            cache[slot, 1],
            preferred_element_type=F32,
        )
        for head in range(4):
            columns = slice(head * HD, (head + 1) * HD)
            carry[slot : slot + 1, columns] = mixed[head : head + 1]
            carry[REQS + slot : REQS + slot + 1, columns] = mixed[4 + head : 5 + head]
    row_at = lax.broadcasted_iota(jnp.int32, (REQS, wide), 0)
    gone = row_at < 0
    for move in range(MOVES):
        gone = gone | (row_at == moving[move, me])
    dead = gone & (jnp.broadcast_to(sender.astype(jnp.int32), gone.shape) == 1)
    carry[REQS : 2 * REQS, :] = jnp.where(dead, 0.0, carry[REQS : 2 * REQS, :])
    for copy in load([(carry, carry_hbm, carry_sem)]) + parcels:
        copy.wait()


def unpack_kernel(
    lengths_hbm,
    pairing_hbm,
    moving_hbm,
    parcel_hbm,
    arrived_out,
    lengths,
    pairing,
    moving,
    parcel,
    arrived,
    fact_sem,
    parcel_sem,
    arrived_sem,
):
    facts = load(
        [
            (lengths_hbm, lengths, fact_sem.at[0]),
            (pairing_hbm, pairing, fact_sem.at[1]),
            (moving_hbm, moving, fact_sem.at[2]),
        ]
    )
    parcels = load([(parcel_hbm, parcel.at[pl.ds(0, PARCEL)], parcel_sem)])
    for copy in facts:
        copy.wait()
    me, partner, sender = role(lengths, pairing)
    for copy in parcels:
        copy.wait()
    row_at = lax.broadcasted_iota(jnp.int32, (SPAN, HD), 0)
    offset = 0
    arrivals = []
    for move in range(MOVES):
        end = lengths[moving[move, partner], partner]
        size = (end // TILE + 1) * TILE
        last = jnp.where(sender, -1, end)
        for kind in range(2):
            start = pl.multiple_of(offset + kind * size, TILE)
            block = parcel[pl.ds(start, SPAN), :].astype(F32)
            arrived[move, kind] = jnp.where(row_at <= last, block, 0.0).astype(BF16)
        offset = offset + 2 * size
        arrivals += load([(arrived.at[move], arrived_out.at[move], arrived_sem.at[move])])
    for copy in arrivals:
        copy.wait()


def out_kernel(
    carry_hbm,
    arrived_hbm,
    out_weight,
    first_out,
    second_out,
    carry,
    weight_held,
    cache,
    scores,
    part,
    from_x,
    total,
    from_z,
    whole,
    fact_sem,
    weight_sem,
    x_send,
    x_recv,
    z_send,
    z_recv,
    g_send,
    g_recv,
):
    inst = lax.axis_index("inst")
    lane = lax.axis_index("tp")
    x = lane // 2
    z = lane % 2
    x_peers = [(inst, lax.rem(x + step, 4) * 2 + z) for step in range(1, 4)]
    z_peer = (inst, x * 2 + 1 - z)
    barrier = pltpu.get_barrier_semaphore()
    for peer in [z_peer] + x_peers:
        pl.semaphore_signal(barrier, inc=1, device_id=peer, device_id_type=MESH)
    width = weight_held.shape[2]
    quarter = width // 4
    order = (2, 1, 3, 0)
    facts = load([(carry_hbm, carry, fact_sem.at[0]), (arrived_hbm, cache, fact_sem.at[1])])
    weights = load(
        [
            (
                out_weight.at[:, pl.ds(pl.multiple_of(lax.rem(x + step, 4) * width, width), width)],
                weight_held.at[step],
                weight_sem.at[step],
            )
            for step in order
        ]
    )

    for copy in facts:
        copy.wait()
    row_at = lax.broadcasted_iota(jnp.int32, (SPAN, HD), 0).astype(F32)
    lane_at = lax.broadcasted_iota(jnp.int32, (8, SPAN), 1).astype(F32)
    for move in range(MOVES):
        own = slice(ROWS + 8 + move, ROWS + 9 + move)
        here = row_at == carry[own, 2 * HD : 3 * HD]
        for kind in range(2):
            fresh = jnp.broadcast_to(carry[own, HD * kind : HD * (kind + 1)], here.shape)
            cache[move, kind] = jnp.where(here, fresh, cache[move, kind].astype(F32)).astype(BF16)
        rows = jnp.concatenate(
            [
                carry[ROWS + move : ROWS + move + 1, HD * head : HD * (head + 1)]
                for head in range(4)
            ]
            + [jnp.zeros((4, HD), F32)],
            axis=0,
        )
        raw = lax.dot_general(
            rows.astype(BF16),
            cache[move, 0],
            (((1,), (1,)), ((), ())),
            preferred_element_type=F32,
        ) * (1.0 / math.sqrt(HD))
        limit = jnp.broadcast_to(carry[own, 2 * HD : 2 * HD + 1], raw.shape)
        scores[8 * move : 8 * move + 8, :] = jnp.where(lane_at <= limit, raw, -jnp.inf)
    scores[...] = softmax_rows(scores[...])
    for move in range(MOVES):
        mixed = jnp.dot(
            scores[8 * move : 8 * move + 8, :].astype(BF16),
            cache[move, 1],
            preferred_element_type=F32,
        )
        receives = jnp.broadcast_to(
            carry[ROWS + 8 + move : ROWS + 9 + move, 3 * HD :], mixed.shape
        )
        mixed = jnp.where(receives > 0.5, mixed, 0.0)
        for head in range(4):
            carry[2 * REQS + move : 2 * REQS + move + 1, HD * head : HD * (head + 1)] = mixed[
                head : head + 1
            ]

    rows = carry[:ROWS, :].astype(BF16)
    for turn, step in enumerate(order):
        weights[turn].wait()
        block = jnp.dot(rows, weight_held[step], preferred_element_type=F32)
        part[step, :, :width] = block[:REQS]
        part[step, :, width : 2 * width] = block[REQS : 2 * REQS]
        for at in range(4):
            part[step, 4 * at : 4 * at + 4, 2 * width :] = block[
                2 * REQS : 2 * REQS + MOVES, quarter * at : quarter * (at + 1)
            ]
    pl.semaphore_wait(barrier, 4)
    edges = (0,) + SPLITS
    pieces = [slice(low, high) for low, high in zip(edges[:-1], edges[1:])]
    x_copies = {}
    z_copies = []
    g_copies = []
    def scatter(index):
        for step in order[:3]:
            copy = pltpu.make_async_remote_copy(
                src_ref=part.at[step, :, pieces[index]],
                dst_ref=from_x.at[step - 1, :, pieces[index]],
                send_sem=x_send.at[index, step - 1],
                recv_sem=x_recv.at[index, step - 1],
                device_id=x_peers[step - 1],
                device_id_type=MESH,
            )
            copy.start()
            x_copies[index, step] = copy

    scatter(0)
    for index, columns in enumerate(pieces):
        if index + 1 < len(pieces):
            scatter(index + 1)
        for step in order[:3]:
            x_copies[index, step].wait_recv()
        total[:, columns] = (part[0, :, columns] + from_x[0, :, columns]) + (
            from_x[1, :, columns] + from_x[2, :, columns]
        )
        copy = pltpu.make_async_remote_copy(
            src_ref=total.at[:, columns],
            dst_ref=from_z.at[:, columns],
            send_sem=z_send.at[index],
            recv_sem=z_recv.at[index],
            device_id=z_peer,
            device_id_type=MESH,
        )
        copy.start()
        z_copies.append(copy)
    for index, columns in enumerate(pieces):
        z_copies[index].wait_recv()
        whole[x, :, columns] = (total[:, columns] + from_z[:, columns]).astype(BF16)
        for step in order[:3]:
            copy = pltpu.make_async_remote_copy(
                src_ref=whole.at[x, :, columns],
                dst_ref=whole.at[x, :, columns],
                send_sem=g_send.at[index, step - 1],
                recv_sem=g_recv.at[index, step - 1],
                device_id=x_peers[step - 1],
                device_id_type=MESH,
            )
            copy.start()
            g_copies.append(copy)
    for copy in g_copies:
        copy.wait_recv()
    for chunk in range(4):
        columns = slice(chunk * width, (chunk + 1) * width)
        first_out[:, columns] = whole[chunk, :, :width]
        second_out[:REQS, columns] = whole[chunk, :, width : 2 * width]
        folded = whole[chunk, :, 2 * width :].astype(F32)
        spread = [folded[4 * at : 4 * at + 4] for at in range(4)]
        second_out[REQS:, columns] = jnp.concatenate(spread, axis=1).astype(BF16)
    for copy in list(x_copies.values()) + z_copies + g_copies:
        copy.wait_send()


def finish_kernel(first_in, second_in, first_out, second_out, first, second, in_sem, out_sem):
    reads = load([(first_in, first, in_sem.at[0]), (second_in, second, in_sem.at[1])])
    writes = []
    for index, pair in enumerate(((first, first_out), (second, second_out))):
        reads[index].wait()
        writes += load([pair + (out_sem.at[index],)])
    for copy in writes:
        copy.wait()


def route(bit, upward):
    pairs = []
    for low in range(32):
        high = low | 1 << bit
        if high != low:
            pairs.append((low, high) if upward else (high, low))
    return pairs


def send_branch(bit, upward, size, parcel):
    moved = lax.ppermute(parcel[: size * STRIDE], "inst", route(bit, upward))
    return lax.dynamic_update_slice(parcel, moved, (0, 0))


def body(
    tokens_now,
    tokens_next,
    norm_gain,
    query_weight,
    key_weight,
    value_weight,
    out_weight,
    kv_cache,
    lengths,
    pairing,
    moving,
):
    vmem = pl.BlockSpec(memory_space=pltpu.VMEM)
    smem = pl.BlockSpec(memory_space=pltpu.SMEM)
    hbm = pl.BlockSpec(memory_space=pl.ANY)
    params = pltpu.CompilerParams(vmem_limit_bytes=LIMIT)
    d = tokens_now.shape[-1]
    wide = query_weight.shape[1]
    stored = kv_cache[0]
    half = ROPE_THETA ** (-(np.arange(HD // 2, dtype=np.float32) * 2.0) / HD)
    frequency = np.concatenate([half, half]).astype(np.float32)[None, :]
    shape = jax.ShapeDtypeStruct
    dma = pltpu.SemaphoreType.DMA
    facts = (lengths.T, pairing, moving.T)
    fact_room = [pltpu.SMEM(fact.shape, jnp.int32) for fact in facts]
    carried = (ROWS + 16, wide)
    parcel, carry, way, size_class = pl.pallas_call(
        front_kernel,
        out_shape=(
            shape((PARCEL, HD), BF16),
            shape(carried, F32),
            shape((1,), jnp.int32),
            shape((1,), jnp.int32),
        ),
        in_specs=[hbm] * 11,
        out_specs=(hbm, hbm, smem, smem),
        scratch_shapes=fact_room
        + [
            pltpu.VMEM((1, HD), F32),
            pltpu.VMEM((REQS, d), BF16),
            pltpu.VMEM((REQS + MOVES, d), BF16),
            pltpu.VMEM((1, d), F32),
            pltpu.VMEM((d, HD), BF16),
            pltpu.VMEM((d, HD), BF16),
            pltpu.VMEM((d, wide), BF16),
            pltpu.VMEM(stored.shape, BF16),
            pltpu.VMEM((ROWS, d), BF16),
            pltpu.VMEM((ROWS, HD), F32),
            pltpu.VMEM((ROWS, HD), F32),
            pltpu.VMEM((8 * REQS, HD), F32),
            pltpu.VMEM((8 * REQS, SPAN), F32),
            pltpu.VMEM(carried, F32),
            dma((4,)),
            dma((3,)),
            dma((2,)),
            dma((4,)),
            dma((REQS,)),
            dma((2 * MOVES,)),
            dma,
        ],
        compiler_params=params,
        name="front",
    )(
        *facts,
        frequency,
        tokens_now[0],
        tokens_next[0],
        norm_gain[None, :],
        key_weight,
        value_weight,
        query_weight,
        stored,
    )

    def sized(bit, upward, parcel, size_class):
        sends = [functools.partial(send_branch, bit, upward, size) for size in range(1, SIZES + 1)]
        return lax.switch(size_class, sends, parcel)

    ways = [functools.partial(sized, bit, upward) for bit in range(5) for upward in (0, 1)]
    moved = lax.switch(way[0], ways, parcel, size_class[0])
    arrival = (MOVES, 2, SPAN, HD)
    arrived = pl.pallas_call(
        unpack_kernel,
        out_shape=shape(arrival, BF16),
        in_specs=[hbm] * 4,
        out_specs=hbm,
        scratch_shapes=fact_room
        + [
            pltpu.VMEM((PARCEL + SPAN, HD), BF16),
            pltpu.VMEM(arrival, BF16),
            dma((3,)),
            dma,
            dma((MOVES,)),
        ],
        compiler_params=params,
        name="unpack",
    )(*facts, moved)
    width = d // 4
    side = 2 * width + width // 4
    count = len(SPLITS)
    outs = (shape((REQS, d), BF16), shape((REQS + MOVES, d), BF16))
    raw = pl.pallas_call(
        out_kernel,
        out_shape=outs,
        in_specs=[hbm] * 3,
        out_specs=(vmem, vmem),
        scratch_shapes=[
            pltpu.VMEM(carried, F32),
            pltpu.VMEM((4, wide, width), BF16),
            pltpu.VMEM(arrival, BF16),
            pltpu.VMEM((8 * MOVES, SPAN), F32),
            pltpu.VMEM((4, REQS, side), F32),
            pltpu.VMEM((3, REQS, side), F32),
            pltpu.VMEM((REQS, side), F32),
            pltpu.VMEM((REQS, side), F32),
            pltpu.VMEM((4, REQS, side), BF16),
            dma((2,)),
            dma((4,)),
            dma((count, 3)),
            dma((count, 3)),
            dma((count,)),
            dma((count,)),
            dma((count, 3)),
            dma((count, 3)),
        ],
        compiler_params=pltpu.CompilerParams(
            vmem_limit_bytes=LIMIT, collective_id=0, has_side_effects=True
        ),
        name="project_out",
    )(carry, arrived, out_weight)
    first, second = pl.pallas_call(
        finish_kernel,
        out_shape=outs,
        in_specs=[hbm] * 2,
        out_specs=(hbm, hbm),
        scratch_shapes=[pltpu.VMEM(out.shape, BF16) for out in outs] + [dma((2,)), dma((2,))],
        compiler_params=params,
        name="finish",
    )(*raw)
    return first[None], second[None], arrived[None]


def solution(mesh):
    in_specs = (
        P("inst", None, None),
        P("inst", None, None),
        P(),
        P(None, "tp"),
        P(None, "tp"),
        P(None, "tp"),
        P("tp", None),
        P("inst", None, None, None, "tp"),
        P(),
        P(),
        P(),
    )
    out_specs = (P("inst", None, None), P("inst", None, None), P("inst", None, None, None, "tp"))
    return jax.shard_map(body, mesh=mesh, in_specs=in_specs, out_specs=out_specs, check_vma=False)
```

```python
import functools
import math

import jax
import jax.numpy as jnp
import numpy as np
from jax import lax
from jax.experimental import pallas as pl
from jax.experimental.pallas import tpu as pltpu
from jax.sharding import PartitionSpec as P

HD = 128
ROPE_THETA = 500000.0
NORM_EPSILON = 1e-05
MESH = pl.DeviceIdType.MESH
F32 = jnp.float32
BF16 = jnp.bfloat16
LIMIT = 60 * 1024 * 1024

ROWS = 48
REQS = 16
MOVES = 4
SPAN = 480
TILE = 16
PARCEL = MOVES * SPAN
SIZES = 4
STRIDE = PARCEL // SIZES
SPLITS = (1024, 2304)


def role(lengths, pairing):
    me = lax.axis_index("inst")
    partner = pairing[me]
    mine = lengths[0, me]
    theirs = lengths[0, partner]
    for slot in range(1, REQS):
        mine = mine + lengths[slot, me]
        theirs = theirs + lengths[slot, partner]
    sender = (mine > theirs) | ((mine == theirs) & (me < partner))
    return me, partner, sender


def load(copies):
    started = []
    for source, target, semaphore in copies:
        copy = pltpu.make_async_copy(source, target, semaphore)
        copy.start()
        started.append(copy)
    return started


def softmax_rows(scores):
    largest = jnp.max(scores, axis=-1, keepdims=True)
    raised = jnp.exp(scores - largest)
    return raised / jnp.sum(raised, axis=-1, keepdims=True)


def score_block(query, keys, limit):
    scores = lax.dot_general(
        query.astype(BF16), keys, (((1,), (1,)), ((), ())), preferred_element_type=F32
    ) * (1.0 / math.sqrt(HD))
    lane_at = lax.broadcasted_iota(jnp.int32, scores.shape, 1)
    return jnp.where(lane_at <= limit, scores, -jnp.inf)


def front_kernel(
    lengths_hbm,
    pairing_hbm,
    moving_hbm,
    frequency_hbm,
    tokens_now_hbm,
    tokens_next_hbm,
    norm_gain_hbm,
    key_weight,
    value_weight,
    query_weight,
    kv_cache,
    parcel_hbm,
    carry_hbm,
    way_out,
    size_out,
    lengths,
    pairing,
    moving,
    frequency,
    tokens_now,
    tokens_next,
    norm_gain,
    key_held,
    value_held,
    query_held,
    cache,
    normed,
    new_key,
    new_value,
    query,
    scores,
    carry,
    fact_sem,
    token_sem,
    weight_sem,
    query_sem,
    cache_sem,
    parcel_sem,
    carry_sem,
):
    facts = load(
        [
            (lengths_hbm, lengths, fact_sem.at[0]),
            (pairing_hbm, pairing, fact_sem.at[1]),
            (moving_hbm, moving, fact_sem.at[2]),
            (frequency_hbm, frequency, fact_sem.at[3]),
        ]
    )
    tokens = load(
        [
            (tokens_now_hbm, tokens_now, token_sem.at[0]),
            (tokens_next_hbm, tokens_next, token_sem.at[1]),
            (norm_gain_hbm, norm_gain, token_sem.at[2]),
        ]
    )
    weights = load(
        [
            (key_weight, key_held, weight_sem.at[0]),
            (value_weight, value_held, weight_sem.at[1]),
        ]
    )
    for slot in range(REQS):
        cache[slot, 1] = jnp.zeros((SPAN, HD), BF16)
    for copy in facts:
        copy.wait()
    me, partner, sender = role(lengths, pairing)
    caches = []
    for slot in range(REQS):
        size = pl.multiple_of(((lengths[slot, me] + 1) // TILE + 1) * TILE, TILE)
        caches.append(
            (
                kv_cache.at[slot, :, pl.ds(0, size)],
                cache.at[slot, :, pl.ds(0, size)],
                cache_sem.at[slot],
            )
        )
    caches = load(caches)
    depth = query_held.shape[0] // 4
    queries = load(
        [
            (
                query_weight.at[pl.ds(depth * part, depth)],
                query_held.at[pl.ds(depth * part, depth)],
                query_sem.at[part],
            )
            for part in range(4)
        ]
    )
    total = 0
    giver = jnp.where(sender, me, partner)
    for move in range(MOVES):
        total = total + (lengths[moving[move, giver], giver] // TILE + 1) * TILE
    distance = me ^ partner
    bit = (
        (distance >= 2).astype(jnp.int32)
        + (distance >= 4).astype(jnp.int32)
        + (distance >= 8).astype(jnp.int32)
        + (distance >= 16).astype(jnp.int32)
    )
    upward = (sender == (me < partner)).astype(jnp.int32)
    way_out[0] = bit * 2 + upward
    size_out[0] = (total + STRIDE - 1) // STRIDE - 1

    row_at = lax.broadcasted_iota(jnp.int32, (ROWS, HD), 0)
    times = jnp.zeros((ROWS, HD), jnp.int32)
    for slot in range(REQS):
        times = jnp.where(row_at == slot, lengths[slot, me], times)
        times = jnp.where(row_at == REQS + slot, lengths[slot, me] + 1, times)
    for move in range(MOVES):
        in_length = lengths[moving[move, partner], partner]
        times = jnp.where(row_at == 2 * REQS + move, in_length + 1, times)
    angles = times.astype(F32) * frequency[...]
    lane_at = lax.broadcasted_iota(jnp.int32, (ROWS, HD), 1)
    cosine = jnp.cos(angles)
    sine = jnp.sin(angles)
    sine = jnp.where(lane_at < HD // 2, -sine, sine)

    for copy in tokens:
        copy.wait()
    gain = norm_gain[...]
    normed[2 * REQS :, :] = jnp.zeros((ROWS - 2 * REQS, normed.shape[1]), BF16)
    for rows, base in ((tokens_now, 0), (tokens_next, REQS)):
        count = rows.shape[0]
        widened = rows[...].astype(F32)
        scale = lax.rsqrt(jnp.mean(widened * widened, axis=-1, keepdims=True) + NORM_EPSILON)
        normed[base : base + count, :] = (widened * scale * gain).astype(BF16)

    for copy in weights:
        copy.wait()
    key = jnp.dot(normed[...], key_held[...], preferred_element_type=F32)
    value = jnp.dot(normed[...], value_held[...], preferred_element_type=F32)
    key = key * cosine + pltpu.roll(key, HD // 2, 1) * sine
    new_key[...] = key.astype(BF16).astype(F32)
    new_value[...] = value.astype(BF16).astype(F32)

    for slot in range(REQS):
        caches[slot].wait()
    window_at = lax.broadcasted_iota(jnp.int32, (2 * TILE, HD), 0)
    for group in range(0, REQS, 4):
        changed = []
        for slot in range(group, group + 4):
            length = lengths[slot, me]
            base = pl.multiple_of(jnp.minimum(length // TILE * TILE, SPAN - 2 * TILE), TILE)
            for kind, fresh in ((0, new_key), (1, new_value)):
                at = (slot, kind, pl.ds(base, 2 * TILE), slice(None))
                held = cache[at].astype(F32)
                for row, place in ((slot, length), (REQS + slot, length + 1)):
                    held = jnp.where(
                        window_at == place - base,
                        jnp.broadcast_to(fresh[row : row + 1, :], held.shape),
                        held,
                    )
                changed.append((at, held.astype(BF16)))
        for at, held in changed:
            cache[at] = held
    offset = 0
    parcels = []
    for move in range(MOVES):
        slot = moving[move, me]
        size = pl.multiple_of((lengths[slot, me] // TILE + 1) * TILE, TILE)
        start = pl.multiple_of(offset, TILE)
        for kind in range(2):
            parcels.append(
                (
                    cache.at[slot, kind, pl.ds(0, size)],
                    parcel_hbm.at[pl.ds(start, size), HD * kind : HD * (kind + 1)],
                    parcel_sem.at[2 * move + kind],
                )
            )
        offset = offset + size
    parcels = load(parcels)

    wide = query_held.shape[1]
    total = jnp.zeros((ROWS, wide), F32)
    for part in range(4):
        queries[part].wait()
        columns = slice(depth * part, depth * (part + 1))
        total = total + jnp.dot(
            normed[:, columns], query_held[columns, :], preferred_element_type=F32
        )
    carry[...] = jnp.zeros(carry.shape, F32)
    for head in range(4):
        columns = slice(head * HD, (head + 1) * HD)
        part = total[:, columns]
        part = part * cosine + pltpu.roll(part, HD // 2, 1) * sine
        part = part.astype(BF16).astype(F32)
        for slot in range(REQS):
            query[8 * slot + head : 8 * slot + head + 1, :] = part[slot : slot + 1]
            query[8 * slot + 4 + head : 8 * slot + 5 + head, :] = part[REQS + slot : REQS + slot + 1]
        for move in range(MOVES):
            at = ROWS + 4 * move + head
            carry[at : at + 1, :HD] = part[2 * REQS + move : 2 * REQS + move + 1]
    spot = lax.broadcasted_iota(jnp.int32, (4, HD), 1)
    receives = jnp.logical_not(sender).astype(jnp.int32)
    first = 0
    for move in range(MOVES):
        rows = slice(ROWS + 4 * move, ROWS + 4 * move + 4)
        own = slice(2 * REQS + move, 2 * REQS + move + 1)
        carry[rows, HD : 2 * HD] = jnp.broadcast_to(new_key[own, :], (4, HD))
        carry[rows, 2 * HD : 3 * HD] = jnp.broadcast_to(new_value[own, :], (4, HD))
        end = lengths[moving[move, partner], partner]
        marks = jnp.where(spot == 0, first, jnp.where(spot == 1, first + end, receives))
        carry[rows, 3 * HD :] = marks.astype(F32)
        first = first + (end // TILE + 1) * TILE
    late = (lax.broadcasted_iota(jnp.int32, (8, SPAN), 0) >= 4).astype(jnp.int32)
    for slot in range(REQS):
        scores[8 * slot : 8 * slot + 8, :] = score_block(
            query[8 * slot : 8 * slot + 8, :], cache[slot, 0], lengths[slot, me] + late
        )
    for group in range(4):
        rows = slice(32 * group, 32 * group + 32)
        scores[rows, :] = softmax_rows(scores[rows, :])
    for slot in range(REQS):
        mixed = jnp.dot(
            scores[8 * slot : 8 * slot + 8, :].astype(BF16),
            cache[slot, 1],
            preferred_element_type=F32,
        )
        for head in range(4):
            columns = slice(head * HD, (head + 1) * HD)
            carry[slot : slot + 1, columns] = mixed[head : head + 1]
            carry[REQS + slot : REQS + slot + 1, columns] = mixed[4 + head : 5 + head]
    row_at = lax.broadcasted_iota(jnp.int32, (REQS, wide), 0)
    gone = row_at < 0
    for move in range(MOVES):
        gone = gone | (row_at == moving[move, me])
    dead = gone & (jnp.broadcast_to(sender.astype(jnp.int32), gone.shape) == 1)
    carry[REQS : 2 * REQS, :] = jnp.where(dead, 0.0, carry[REQS : 2 * REQS, :])
    for copy in load([(carry, carry_hbm, carry_sem)]) + parcels:
        copy.wait()


def out_kernel(
    carry_hbm,
    parcel_hbm,
    out_weight,
    first_out,
    second_out,
    carry,
    weight_held,
    parcel,
    part,
    from_x,
    total,
    from_z,
    whole,
    fact_sem,
    weight_sem,
    x_send,
    x_recv,
    z_send,
    z_recv,
    g_send,
    g_recv,
):
    inst = lax.axis_index("inst")
    lane = lax.axis_index("tp")
    x = lane // 2
    z = lane % 2
    x_peers = [(inst, lax.rem(x + step, 4) * 2 + z) for step in range(1, 4)]
    z_peer = (inst, x * 2 + 1 - z)
    barrier = pltpu.get_barrier_semaphore()
    for peer in [z_peer] + x_peers:
        pl.semaphore_signal(barrier, inc=1, device_id=peer, device_id_type=MESH)
    width = weight_held.shape[2]
    quarter = width // 4
    order = (2, 1, 3, 0)
    facts = load([(carry_hbm, carry, fact_sem.at[0]), (parcel_hbm, parcel, fact_sem.at[1])])
    weights = load(
        [
            (
                out_weight.at[:, pl.ds(pl.multiple_of(lax.rem(x + step, 4) * width, width), width)],
                weight_held.at[step],
                weight_sem.at[step],
            )
            for step in order
        ]
    )

    facts[0].wait()
    rows = carry[:REQS, :].astype(BF16)
    for turn, step in enumerate(order):
        weights[turn].wait()
        part[step, :, :width] = jnp.dot(rows, weight_held[step], preferred_element_type=F32)
    edges = (0,) + SPLITS
    pieces = [slice(low, high) for low, high in zip(edges[:-1], edges[1:])]
    x_copies = {}
    z_copies = []
    g_copies = []
    def scatter(index):
        for step in order[:3]:
            copy = pltpu.make_async_remote_copy(
                src_ref=part.at[step, :, pieces[index]],
                dst_ref=from_x.at[step - 1, :, pieces[index]],
                send_sem=x_send.at[index, step - 1],
                recv_sem=x_recv.at[index, step - 1],
                device_id=x_peers[step - 1],
                device_id_type=MESH,
            )
            copy.start()
            x_copies[index, step] = copy

    pl.semaphore_wait(barrier, 4)
    scatter(0)

    facts[1].wait()
    query = carry[ROWS:, :HD]
    own_value = carry[ROWS:, 2 * HD : 3 * HD]
    scores = lax.dot_general(
        query.astype(BF16),
        parcel[:, :HD],
        (((1,), (1,)), ((), ())),
        preferred_element_type=F32,
    ) * (1.0 / math.sqrt(HD))
    lane_at = lax.broadcasted_iota(jnp.int32, scores.shape, 1).astype(F32)
    begin = jnp.broadcast_to(carry[ROWS:, 3 * HD : 3 * HD + 1], scores.shape)
    end = jnp.broadcast_to(carry[ROWS:, 3 * HD + 1 : 3 * HD + 2], scores.shape)
    scores = jnp.where((lane_at >= begin) & (lane_at <= end), scores, -jnp.inf)
    own_score = jnp.sum(query * carry[ROWS:, HD : 2 * HD], axis=-1, keepdims=True) * (
        1.0 / math.sqrt(HD)
    )
    largest = jnp.maximum(jnp.max(scores, axis=-1, keepdims=True), own_score)
    raised = jnp.exp(scores - largest)
    own_raised = jnp.exp(own_score - largest)
    below = jnp.sum(raised, axis=-1, keepdims=True) + own_raised
    own_weight = (own_raised / below).astype(BF16).astype(F32)
    mixed = jnp.dot(
        (raised / below).astype(BF16), parcel[:, HD:], preferred_element_type=F32
    ) + own_weight * own_value
    receives = jnp.broadcast_to(carry[ROWS:, 3 * HD + 2 : 3 * HD + 3], mixed.shape)
    mixed = jnp.where(receives > 0.5, mixed, 0.0)
    for move in range(MOVES):
        for head in range(4):
            at = 4 * move + head
            carry[2 * REQS + move : 2 * REQS + move + 1, HD * head : HD * (head + 1)] = mixed[
                at : at + 1
            ]

    rows = carry[REQS:ROWS, :].astype(BF16)
    for step in order:
        block = jnp.dot(rows, weight_held[step], preferred_element_type=F32)
        part[step, :, width : 2 * width] = block[:REQS]
        for at in range(4):
            part[step, 4 * at : 4 * at + 4, 2 * width :] = block[
                REQS : REQS + MOVES, quarter * at : quarter * (at + 1)
            ]
    scatter(1)
    for index, columns in enumerate(pieces):
        for step in order[:3]:
            x_copies[index, step].wait_recv()
        total[:, columns] = (part[0, :, columns] + from_x[0, :, columns]) + (
            from_x[1, :, columns] + from_x[2, :, columns]
        )
        copy = pltpu.make_async_remote_copy(
            src_ref=total.at[:, columns],
            dst_ref=from_z.at[:, columns],
            send_sem=z_send.at[index],
            recv_sem=z_recv.at[index],
            device_id=z_peer,
            device_id_type=MESH,
        )
        copy.start()
        z_copies.append(copy)
    for index, columns in enumerate(pieces):
        z_copies[index].wait_recv()
        whole[x, :, columns] = (total[:, columns] + from_z[:, columns]).astype(BF16)
        for step in order[:3]:
            copy = pltpu.make_async_remote_copy(
                src_ref=whole.at[x, :, columns],
                dst_ref=whole.at[x, :, columns],
                send_sem=g_send.at[index, step - 1],
                recv_sem=g_recv.at[index, step - 1],
                device_id=x_peers[step - 1],
                device_id_type=MESH,
            )
            copy.start()
            g_copies.append(copy)
    for copy in g_copies:
        copy.wait_recv()
    for chunk in range(4):
        columns = slice(chunk * width, (chunk + 1) * width)
        first_out[:, columns] = whole[chunk, :, :width]
        second_out[:REQS, columns] = whole[chunk, :, width : 2 * width]
        folded = whole[chunk, :, 2 * width :].astype(F32)
        spread = [folded[4 * at : 4 * at + 4] for at in range(4)]
        second_out[REQS:, columns] = jnp.concatenate(spread, axis=1).astype(BF16)
    for copy in list(x_copies.values()) + z_copies + g_copies:
        copy.wait_send()


def finish_kernel(
    lengths_hbm,
    pairing_hbm,
    moving_hbm,
    parcel_hbm,
    first_in,
    second_in,
    first_out,
    second_out,
    arrived_out,
    lengths,
    pairing,
    moving,
    parcel,
    first,
    second,
    arrived,
    fact_sem,
    in_sem,
    out_sem,
    arrived_sem,
):
    facts = load(
        [
            (lengths_hbm, lengths, fact_sem.at[0]),
            (pairing_hbm, pairing, fact_sem.at[1]),
            (moving_hbm, moving, fact_sem.at[2]),
        ]
    )
    reads = load(
        [
            (parcel_hbm, parcel.at[pl.ds(0, PARCEL)], in_sem.at[0]),
            (first_in, first, in_sem.at[1]),
            (second_in, second, in_sem.at[2]),
        ]
    )
    for copy in facts:
        copy.wait()
    me, partner, sender = role(lengths, pairing)
    reads[0].wait()
    row_at = lax.broadcasted_iota(jnp.int32, (SPAN, HD), 0)
    offset = 0
    writes = []
    for move in range(MOVES):
        end = lengths[moving[move, partner], partner]
        last = jnp.where(sender, -1, end)
        start = pl.multiple_of(offset, TILE)
        for kind in range(2):
            block = parcel[pl.ds(start, SPAN), HD * kind : HD * (kind + 1)].astype(F32)
            arrived[move, kind] = jnp.where(row_at <= last, block, 0.0).astype(BF16)
        offset = offset + (end // TILE + 1) * TILE
        writes += load([(arrived.at[move], arrived_out.at[move], arrived_sem.at[move])])
    for index, pair in enumerate(((first, first_out), (second, second_out))):
        reads[index + 1].wait()
        writes += load([pair + (out_sem.at[index],)])
    for copy in writes:
        copy.wait()


def route(bit, upward):
    pairs = []
    for low in range(32):
        high = low | 1 << bit
        if high != low:
            pairs.append((low, high) if upward else (high, low))
    return pairs


def body(
    tokens_now,
    tokens_next,
    norm_gain,
    query_weight,
    key_weight,
    value_weight,
    out_weight,
    kv_cache,
    lengths,
    pairing,
    moving,
):
    vmem = pl.BlockSpec(memory_space=pltpu.VMEM)
    smem = pl.BlockSpec(memory_space=pltpu.SMEM)
    hbm = pl.BlockSpec(memory_space=pl.ANY)
    params = pltpu.CompilerParams(vmem_limit_bytes=LIMIT)
    d = tokens_now.shape[-1]
    wide = query_weight.shape[1]
    stored = kv_cache[0]
    half = ROPE_THETA ** (-(np.arange(HD // 2, dtype=np.float32) * 2.0) / HD)
    frequency = np.concatenate([half, half]).astype(np.float32)[None, :]
    shape = jax.ShapeDtypeStruct
    dma = pltpu.SemaphoreType.DMA
    facts = (lengths.T, pairing, moving.T)
    fact_room = [pltpu.SMEM(fact.shape, jnp.int32) for fact in facts]
    carried = (ROWS + 16, wide)
    parcel, carry, way, size_class = pl.pallas_call(
        front_kernel,
        out_shape=(
            shape((PARCEL, 2 * HD), BF16),
            shape(carried, F32),
            shape((1,), jnp.int32),
            shape((1,), jnp.int32),
        ),
        in_specs=[hbm] * 11,
        out_specs=(hbm, hbm, smem, smem),
        scratch_shapes=fact_room
        + [
            pltpu.VMEM((1, HD), F32),
            pltpu.VMEM((REQS, d), BF16),
            pltpu.VMEM((REQS + MOVES, d), BF16),
            pltpu.VMEM((1, d), F32),
            pltpu.VMEM((d, HD), BF16),
            pltpu.VMEM((d, HD), BF16),
            pltpu.VMEM((d, wide), BF16),
            pltpu.VMEM(stored.shape, BF16),
            pltpu.VMEM((ROWS, d), BF16),
            pltpu.VMEM((ROWS, HD), F32),
            pltpu.VMEM((ROWS, HD), F32),
            pltpu.VMEM((8 * REQS, HD), F32),
            pltpu.VMEM((8 * REQS, SPAN), F32),
            pltpu.VMEM(carried, F32),
            dma((4,)),
            dma((3,)),
            dma((2,)),
            dma((4,)),
            dma((REQS,)),
            dma((2 * MOVES,)),
            dma,
        ],
        compiler_params=params,
        name="front",
    )(
        *facts,
        frequency,
        tokens_now[0],
        tokens_next[0],
        norm_gain[None, :],
        key_weight,
        value_weight,
        query_weight,
        stored,
    )

    def sized(size, way, parcel):
        ways = [
            functools.partial(lax.ppermute, axis_name="inst", perm=route(bit, upward))
            for bit in range(5)
            for upward in (0, 1)
        ]
        moved = lax.switch(way, ways, parcel[: size * STRIDE])
        return jnp.pad(moved, ((0, PARCEL - size * STRIDE), (0, 0)))

    sizes = [functools.partial(sized, size) for size in range(1, SIZES + 1)]
    moved = lax.switch(size_class[0], sizes, way[0], parcel)
    width = d // 4
    side = 2 * width + width // 4
    count = len(SPLITS)
    outs = (shape((REQS, d), BF16), shape((REQS + MOVES, d), BF16))
    raw = pl.pallas_call(
        out_kernel,
        out_shape=outs,
        in_specs=[hbm] * 3,
        out_specs=(vmem, vmem),
        scratch_shapes=[
            pltpu.VMEM(carried, F32),
            pltpu.VMEM((4, wide, width), BF16),
            pltpu.VMEM((PARCEL, 2 * HD), BF16),
            pltpu.VMEM((4, REQS, side), F32),
            pltpu.VMEM((3, REQS, side), F32),
            pltpu.VMEM((REQS, side), F32),
            pltpu.VMEM((REQS, side), F32),
            pltpu.VMEM((4, REQS, side), BF16),
            dma((2,)),
            dma((4,)),
            dma((count, 3)),
            dma((count, 3)),
            dma((count,)),
            dma((count,)),
            dma((count, 3)),
            dma((count, 3)),
        ],
        compiler_params=pltpu.CompilerParams(
            vmem_limit_bytes=LIMIT, collective_id=0, has_side_effects=True
        ),
        name="project_out",
    )(carry, moved, out_weight)
    arrival = (MOVES, 2, SPAN, HD)
    first, second, arrived = pl.pallas_call(
        finish_kernel,
        out_shape=outs + (shape(arrival, BF16),),
        in_specs=[hbm] * 6,
        out_specs=(hbm,) * 3,
        scratch_shapes=fact_room
        + [pltpu.VMEM((PARCEL + SPAN, 2 * HD), BF16)]
        + [pltpu.VMEM(out.shape, BF16) for out in outs]
        + [pltpu.VMEM(arrival, BF16), dma((3,)), dma((3,)), dma((2,)), dma((MOVES,))],
        compiler_params=params,
        name="finish",
    )(*facts, moved, *raw)
    return first[None], second[None], arrived[None]


def solution(mesh):
    in_specs = (
        P("inst", None, None),
        P("inst", None, None),
        P(),
        P(None, "tp"),
        P(None, "tp"),
        P(None, "tp"),
        P("tp", None),
        P("inst", None, None, None, "tp"),
        P(),
        P(),
        P(),
    )
    out_specs = (P("inst", None, None), P("inst", None, None), P("inst", None, None, None, "tp"))
    return jax.shard_map(body, mesh=mesh, in_specs=in_specs, out_specs=out_specs, check_vma=False)
```

```python
import functools
import math

import jax
import jax.numpy as jnp
import numpy as np
from jax import lax
from jax.experimental import pallas as pl
from jax.experimental.pallas import tpu as pltpu
from jax.sharding import PartitionSpec as P

HD = 128
ROPE_THETA = 500000.0
NORM_EPSILON = 1e-05
MESH = pl.DeviceIdType.MESH
F32 = jnp.float32
BF16 = jnp.bfloat16
LIMIT = 60 * 1024 * 1024

ROWS = 48
REQS = 16
MOVES = 4
SPAN = 480
TILE = 16
PARCEL = MOVES * SPAN
SIZES = 4
STRIDE = PARCEL // SIZES
SPLITS = (1024, 2304)


def role(lengths, pairing):
    me = lax.axis_index("inst")
    partner = pairing[me]
    mine = lengths[0, me]
    theirs = lengths[0, partner]
    for slot in range(1, REQS):
        mine = mine + lengths[slot, me]
        theirs = theirs + lengths[slot, partner]
    sender = (mine > theirs) | ((mine == theirs) & (me < partner))
    return me, partner, sender


def load(copies):
    started = []
    for source, target, semaphore in copies:
        copy = pltpu.make_async_copy(source, target, semaphore)
        copy.start()
        started.append(copy)
    return started


def softmax_rows(scores):
    largest = jnp.max(scores, axis=-1, keepdims=True)
    raised = jnp.exp(scores - largest)
    return raised / jnp.sum(raised, axis=-1, keepdims=True)


def score_block(query, keys, limit):
    scores = lax.dot_general(
        query.astype(BF16), keys, (((1,), (1,)), ((), ())), preferred_element_type=F32
    ) * (1.0 / math.sqrt(HD))
    lane_at = lax.broadcasted_iota(jnp.int32, scores.shape, 1)
    return jnp.where(lane_at <= limit, scores, -jnp.inf)


def front_kernel(
    lengths_hbm,
    pairing_hbm,
    moving_hbm,
    frequency_hbm,
    tokens_now_hbm,
    tokens_next_hbm,
    norm_gain_hbm,
    key_weight,
    value_weight,
    query_weight,
    kv_cache,
    parcel_hbm,
    carry_hbm,
    way_out,
    lengths,
    pairing,
    moving,
    frequency,
    tokens_now,
    tokens_next,
    norm_gain,
    key_held,
    value_held,
    query_held,
    cache,
    normed,
    new_key,
    new_value,
    query,
    scores,
    carry,
    fact_sem,
    token_sem,
    weight_sem,
    query_sem,
    cache_sem,
    parcel_sem,
    carry_sem,
):
    facts = load(
        [
            (lengths_hbm, lengths, fact_sem.at[0]),
            (pairing_hbm, pairing, fact_sem.at[1]),
            (moving_hbm, moving, fact_sem.at[2]),
            (frequency_hbm, frequency, fact_sem.at[3]),
        ]
    )
    tokens = load(
        [
            (tokens_now_hbm, tokens_now, token_sem.at[0]),
            (tokens_next_hbm, tokens_next, token_sem.at[1]),
            (norm_gain_hbm, norm_gain, token_sem.at[2]),
        ]
    )
    weights = load(
        [
            (key_weight, key_held, weight_sem.at[0]),
            (value_weight, value_held, weight_sem.at[1]),
        ]
    )
    depth = query_held.shape[0] // 4
    queries = load(
        [
            (
                query_weight.at[pl.ds(depth * part, depth)],
                query_held.at[pl.ds(depth * part, depth)],
                query_sem.at[part],
            )
            for part in range(4)
        ]
    )
    for slot in range(REQS):
        cache[slot, 1] = jnp.zeros((SPAN, HD), BF16)
    for copy in facts:
        copy.wait()
    me, partner, sender = role(lengths, pairing)
    caches = []
    for slot in range(REQS):
        size = pl.multiple_of(((lengths[slot, me] + 1) // TILE + 1) * TILE, TILE)
        caches.append(
            (
                kv_cache.at[slot, :, pl.ds(0, size)],
                cache.at[slot, :, pl.ds(0, size)],
                cache_sem.at[slot],
            )
        )
    caches = load(caches)
    total = 0
    giver = jnp.where(sender, me, partner)
    for move in range(MOVES):
        total = total + (lengths[moving[move, giver], giver] // TILE + 1) * TILE
    distance = me ^ partner
    bit = (
        (distance >= 2).astype(jnp.int32)
        + (distance >= 4).astype(jnp.int32)
        + (distance >= 8).astype(jnp.int32)
        + (distance >= 16).astype(jnp.int32)
    )
    upward = (sender == (me < partner)).astype(jnp.int32)
    size_class = (total + STRIDE - 1) // STRIDE - 1
    way_out[0] = (size_class * 5 + bit) * 2 + upward

    row_at = lax.broadcasted_iota(jnp.int32, (ROWS, HD), 0)
    times = jnp.zeros((ROWS, HD), jnp.int32)
    for slot in range(REQS):
        times = jnp.where(row_at == slot, lengths[slot, me], times)
        times = jnp.where(row_at == REQS + slot, lengths[slot, me] + 1, times)
    for move in range(MOVES):
        in_length = lengths[moving[move, partner], partner]
        times = jnp.where(row_at == 2 * REQS + move, in_length + 1, times)
    angles = times.astype(F32) * frequency[...]
    lane_at = lax.broadcasted_iota(jnp.int32, (ROWS, HD), 1)
    cosine = jnp.cos(angles)
    sine = jnp.sin(angles)
    sine = jnp.where(lane_at < HD // 2, -sine, sine)

    for copy in tokens:
        copy.wait()
    gain = norm_gain[...]
    normed[2 * REQS :, :] = jnp.zeros((ROWS - 2 * REQS, normed.shape[1]), BF16)
    for rows, base in ((tokens_now, 0), (tokens_next, REQS)):
        count = rows.shape[0]
        widened = rows[...].astype(F32)
        scale = lax.rsqrt(jnp.mean(widened * widened, axis=-1, keepdims=True) + NORM_EPSILON)
        normed[base : base + count, :] = (widened * scale * gain).astype(BF16)

    for copy in weights:
        copy.wait()
    key = jnp.dot(normed[...], key_held[...], preferred_element_type=F32)
    value = jnp.dot(normed[...], value_held[...], preferred_element_type=F32)
    key = key * cosine + pltpu.roll(key, HD // 2, 1) * sine
    new_key[...] = key.astype(BF16).astype(F32)
    new_value[...] = value.astype(BF16).astype(F32)

    wide = query_held.shape[1]
    total = jnp.zeros((ROWS, wide), F32)
    for part in range(4):
        queries[part].wait()
        columns = slice(depth * part, depth * (part + 1))
        total = total + jnp.dot(
            normed[:, columns], query_held[columns, :], preferred_element_type=F32
        )
    carry[...] = jnp.zeros(carry.shape, F32)
    for head in range(4):
        columns = slice(head * HD, (head + 1) * HD)
        part = total[:, columns]
        part = part * cosine + pltpu.roll(part, HD // 2, 1) * sine
        part = part.astype(BF16).astype(F32)
        for slot in range(REQS):
            query[8 * slot + head : 8 * slot + head + 1, :] = part[slot : slot + 1]
            query[8 * slot + 4 + head : 8 * slot + 5 + head, :] = part[REQS + slot : REQS + slot + 1]
        for move in range(MOVES):
            at = ROWS + 4 * move + head
            carry[at : at + 1, :HD] = part[2 * REQS + move : 2 * REQS + move + 1]
    for slot in range(REQS):
        caches[slot].wait()
    window_at = lax.broadcasted_iota(jnp.int32, (2 * TILE, HD), 0)
    for group in range(0, REQS, 4):
        changed = []
        for slot in range(group, group + 4):
            length = lengths[slot, me]
            base = pl.multiple_of(jnp.minimum(length // TILE * TILE, SPAN - 2 * TILE), TILE)
            for kind, fresh in ((0, new_key), (1, new_value)):
                at = (slot, kind, pl.ds(base, 2 * TILE), slice(None))
                held = cache[at].astype(F32)
                for row, place in ((slot, length), (REQS + slot, length + 1)):
                    held = jnp.where(
                        window_at == place - base,
                        jnp.broadcast_to(fresh[row : row + 1, :], held.shape),
                        held,
                    )
                changed.append((at, held.astype(BF16)))
        for at, held in changed:
            cache[at] = held
    offset = 0
    parcels = []
    for move in range(MOVES):
        slot = moving[move, me]
        size = pl.multiple_of((lengths[slot, me] // TILE + 1) * TILE, TILE)
        start = pl.multiple_of(offset, TILE)
        for kind in range(2):
            parcels.append(
                (
                    cache.at[slot, kind, pl.ds(0, size)],
                    parcel_hbm.at[pl.ds(start, size), HD * kind : HD * (kind + 1)],
                    parcel_sem.at[2 * move + kind],
                )
            )
        offset = offset + size
    parcels = load(parcels)

    spot = lax.broadcasted_iota(jnp.int32, (4, HD), 1)
    receives = jnp.logical_not(sender).astype(jnp.int32)
    first = 0
    for move in range(MOVES):
        rows = slice(ROWS + 4 * move, ROWS + 4 * move + 4)
        own = slice(2 * REQS + move, 2 * REQS + move + 1)
        carry[rows, HD : 2 * HD] = jnp.broadcast_to(new_key[own, :], (4, HD))
        carry[rows, 2 * HD : 3 * HD] = jnp.broadcast_to(new_value[own, :], (4, HD))
        end = lengths[moving[move, partner], partner]
        marks = jnp.where(spot == 0, first, jnp.where(spot == 1, first + end, receives))
        carry[rows, 3 * HD :] = marks.astype(F32)
        first = first + (end // TILE + 1) * TILE
    late = (lax.broadcasted_iota(jnp.int32, (8, SPAN), 0) >= 4).astype(jnp.int32)
    for slot in range(REQS):
        scores[8 * slot : 8 * slot + 8, :] = score_block(
            query[8 * slot : 8 * slot + 8, :], cache[slot, 0], lengths[slot, me] + late
        )
    for group in range(4):
        rows = slice(32 * group, 32 * group + 32)
        scores[rows, :] = softmax_rows(scores[rows, :])
    for slot in range(REQS):
        mixed = jnp.dot(
            scores[8 * slot : 8 * slot + 8, :].astype(BF16),
            cache[slot, 1],
            preferred_element_type=F32,
        )
        for head in range(4):
            columns = slice(head * HD, (head + 1) * HD)
            carry[slot : slot + 1, columns] = mixed[head : head + 1]
            carry[REQS + slot : REQS + slot + 1, columns] = mixed[4 + head : 5 + head]
    row_at = lax.broadcasted_iota(jnp.int32, (REQS, wide), 0)
    gone = row_at < 0
    for move in range(MOVES):
        gone = gone | (row_at == moving[move, me])
    dead = gone & (jnp.broadcast_to(sender.astype(jnp.int32), gone.shape) == 1)
    carry[REQS : 2 * REQS, :] = jnp.where(dead, 0.0, carry[REQS : 2 * REQS, :])
    for copy in load([(carry, carry_hbm, carry_sem)]) + parcels:
        copy.wait()


def out_kernel(
    carry_hbm,
    parcel_hbm,
    out_weight,
    first_out,
    second_out,
    carry,
    weight_held,
    parcel,
    part,
    from_x,
    total,
    from_z,
    whole,
    fact_sem,
    weight_sem,
    x_send,
    x_recv,
    z_send,
    z_recv,
    g_send,
    g_recv,
):
    inst = lax.axis_index("inst")
    lane = lax.axis_index("tp")
    x = lane // 2
    z = lane % 2
    x_peers = [(inst, lax.rem(x + step, 4) * 2 + z) for step in range(1, 4)]
    z_peer = (inst, x * 2 + 1 - z)
    barrier = pltpu.get_barrier_semaphore()
    for peer in [z_peer] + x_peers:
        pl.semaphore_signal(barrier, inc=1, device_id=peer, device_id_type=MESH)
    width = weight_held.shape[2]
    quarter = width // 4
    order = (2, 1, 3, 0)
    facts = load([(carry_hbm, carry, fact_sem.at[0]), (parcel_hbm, parcel, fact_sem.at[1])])
    weights = load(
        [
            (
                out_weight.at[:, pl.ds(pl.multiple_of(lax.rem(x + step, 4) * width, width), width)],
                weight_held.at[step],
                weight_sem.at[step],
            )
            for step in order
        ]
    )

    facts[0].wait()
    rows = carry[:REQS, :].astype(BF16)
    for turn, step in enumerate(order):
        weights[turn].wait()
        part[step, :, :width] = jnp.dot(rows, weight_held[step], preferred_element_type=F32)
    edges = (0,) + SPLITS
    pieces = [slice(low, high) for low, high in zip(edges[:-1], edges[1:])]
    x_copies = {}
    z_copies = []
    g_copies = []
    def scatter(index):
        for step in order[:3]:
            copy = pltpu.make_async_remote_copy(
                src_ref=part.at[step, :, pieces[index]],
                dst_ref=from_x.at[step - 1, :, pieces[index]],
                send_sem=x_send.at[index, step - 1],
                recv_sem=x_recv.at[index, step - 1],
                device_id=x_peers[step - 1],
                device_id_type=MESH,
            )
            copy.start()
            x_copies[index, step] = copy

    pl.semaphore_wait(barrier, 4)
    scatter(0)

    facts[1].wait()
    query = carry[ROWS:, :HD]
    own_value = carry[ROWS:, 2 * HD : 3 * HD]
    scores = lax.dot_general(
        query.astype(BF16),
        parcel[:, :HD],
        (((1,), (1,)), ((), ())),
        preferred_element_type=F32,
    ) * (1.0 / math.sqrt(HD))
    lane_at = lax.broadcasted_iota(jnp.int32, scores.shape, 1).astype(F32)
    begin = jnp.broadcast_to(carry[ROWS:, 3 * HD : 3 * HD + 1], scores.shape)
    end = jnp.broadcast_to(carry[ROWS:, 3 * HD + 1 : 3 * HD + 2], scores.shape)
    scores = jnp.where((lane_at >= begin) & (lane_at <= end), scores, -jnp.inf)
    own_score = jnp.sum(query * carry[ROWS:, HD : 2 * HD], axis=-1, keepdims=True) * (
        1.0 / math.sqrt(HD)
    )
    largest = jnp.maximum(jnp.max(scores, axis=-1, keepdims=True), own_score)
    raised = jnp.exp(scores - largest)
    own_raised = jnp.exp(own_score - largest)
    below = jnp.sum(raised, axis=-1, keepdims=True) + own_raised
    own_weight = (own_raised / below).astype(BF16).astype(F32)
    mixed = jnp.dot(
        (raised / below).astype(BF16), parcel[:, HD:], preferred_element_type=F32
    ) + own_weight * own_value
    receives = jnp.broadcast_to(carry[ROWS:, 3 * HD + 2 : 3 * HD + 3], mixed.shape)
    mixed = jnp.where(receives > 0.5, mixed, 0.0)
    for move in range(MOVES):
        for head in range(4):
            at = 4 * move + head
            carry[2 * REQS + move : 2 * REQS + move + 1, HD * head : HD * (head + 1)] = mixed[
                at : at + 1
            ]

    rows = carry[REQS:ROWS, :].astype(BF16)
    for step in order:
        block = jnp.dot(rows, weight_held[step], preferred_element_type=F32)
        part[step, :, width : 2 * width] = block[:REQS]
        for at in range(4):
            part[step, 4 * at : 4 * at + 4, 2 * width :] = block[
                REQS : REQS + MOVES, quarter * at : quarter * (at + 1)
            ]
    scatter(1)
    for index, columns in enumerate(pieces):
        for step in order[:3]:
            x_copies[index, step].wait_recv()
        total[:, columns] = (part[0, :, columns] + from_x[0, :, columns]) + (
            from_x[1, :, columns] + from_x[2, :, columns]
        )
        copy = pltpu.make_async_remote_copy(
            src_ref=total.at[:, columns],
            dst_ref=from_z.at[:, columns],
            send_sem=z_send.at[index],
            recv_sem=z_recv.at[index],
            device_id=z_peer,
            device_id_type=MESH,
        )
        copy.start()
        z_copies.append(copy)
    for index, columns in enumerate(pieces):
        z_copies[index].wait_recv()
        whole[x, :, columns] = (total[:, columns] + from_z[:, columns]).astype(BF16)
        for step in order[:3]:
            copy = pltpu.make_async_remote_copy(
                src_ref=whole.at[x, :, columns],
                dst_ref=whole.at[x, :, columns],
                send_sem=g_send.at[index, step - 1],
                recv_sem=g_recv.at[index, step - 1],
                device_id=x_peers[step - 1],
                device_id_type=MESH,
            )
            copy.start()
            g_copies.append(copy)
    for copy in g_copies:
        copy.wait_recv()
    for chunk in range(4):
        columns = slice(chunk * width, (chunk + 1) * width)
        first_out[:, columns] = whole[chunk, :, :width]
        second_out[:REQS, columns] = whole[chunk, :, width : 2 * width]
        folded = whole[chunk, :, 2 * width :].astype(F32)
        spread = [folded[4 * at : 4 * at + 4] for at in range(4)]
        second_out[REQS:, columns] = jnp.concatenate(spread, axis=1).astype(BF16)
    for copy in list(x_copies.values()) + z_copies + g_copies:
        copy.wait_send()


def finish_kernel(
    lengths_hbm,
    pairing_hbm,
    moving_hbm,
    parcel_hbm,
    first_in,
    second_in,
    first_out,
    second_out,
    arrived_out,
    lengths,
    pairing,
    moving,
    parcel,
    first,
    second,
    arrived,
    fact_sem,
    in_sem,
    out_sem,
    arrived_sem,
):
    facts = load(
        [
            (lengths_hbm, lengths, fact_sem.at[0]),
            (pairing_hbm, pairing, fact_sem.at[1]),
            (moving_hbm, moving, fact_sem.at[2]),
        ]
    )
    reads = load(
        [
            (parcel_hbm, parcel.at[pl.ds(0, PARCEL)], in_sem.at[0]),
            (first_in, first, in_sem.at[1]),
            (second_in, second, in_sem.at[2]),
        ]
    )
    for copy in facts:
        copy.wait()
    me, partner, sender = role(lengths, pairing)
    reads[0].wait()
    row_at = lax.broadcasted_iota(jnp.int32, (SPAN, HD), 0)
    offset = 0
    writes = []
    for move in range(MOVES):
        end = lengths[moving[move, partner], partner]
        last = jnp.where(sender, -1, end)
        start = pl.multiple_of(offset, TILE)
        for kind in range(2):
            block = parcel[pl.ds(start, SPAN), HD * kind : HD * (kind + 1)].astype(F32)
            arrived[move, kind] = jnp.where(row_at <= last, block, 0.0).astype(BF16)
        offset = offset + (end // TILE + 1) * TILE
        writes += load([(arrived.at[move], arrived_out.at[move], arrived_sem.at[move])])
    for index, pair in enumerate(((first, first_out), (second, second_out))):
        reads[index + 1].wait()
        writes += load([pair + (out_sem.at[index],)])
    for copy in writes:
        copy.wait()


def route(bit, upward):
    pairs = []
    for low in range(32):
        high = low | 1 << bit
        if high != low:
            pairs.append((low, high) if upward else (high, low))
    return pairs


def body(
    tokens_now,
    tokens_next,
    norm_gain,
    query_weight,
    key_weight,
    value_weight,
    out_weight,
    kv_cache,
    lengths,
    pairing,
    moving,
):
    vmem = pl.BlockSpec(memory_space=pltpu.VMEM)
    smem = pl.BlockSpec(memory_space=pltpu.SMEM)
    hbm = pl.BlockSpec(memory_space=pl.ANY)
    params = pltpu.CompilerParams(vmem_limit_bytes=LIMIT)
    d = tokens_now.shape[-1]
    wide = query_weight.shape[1]
    stored = kv_cache[0]
    half = ROPE_THETA ** (-(np.arange(HD // 2, dtype=np.float32) * 2.0) / HD)
    frequency = np.concatenate([half, half]).astype(np.float32)[None, :]
    shape = jax.ShapeDtypeStruct
    dma = pltpu.SemaphoreType.DMA
    facts = (lengths.T, pairing, moving.T)
    fact_room = [pltpu.SMEM(fact.shape, jnp.int32) for fact in facts]
    carried = (ROWS + 16, wide)
    parcel, carry, way = pl.pallas_call(
        front_kernel,
        out_shape=(
            shape((PARCEL, 2 * HD), BF16),
            shape(carried, F32),
            shape((1,), jnp.int32),
        ),
        in_specs=[hbm] * 11,
        out_specs=(hbm, hbm, smem),
        scratch_shapes=fact_room
        + [
            pltpu.VMEM((1, HD), F32),
            pltpu.VMEM((REQS, d), BF16),
            pltpu.VMEM((REQS + MOVES, d), BF16),
            pltpu.VMEM((1, d), F32),
            pltpu.VMEM((d, HD), BF16),
            pltpu.VMEM((d, HD), BF16),
            pltpu.VMEM((d, wide), BF16),
            pltpu.VMEM(stored.shape, BF16),
            pltpu.VMEM((ROWS, d), BF16),
            pltpu.VMEM((ROWS, HD), F32),
            pltpu.VMEM((ROWS, HD), F32),
            pltpu.VMEM((8 * REQS, HD), F32),
            pltpu.VMEM((8 * REQS, SPAN), F32),
            pltpu.VMEM(carried, F32),
            dma((4,)),
            dma((3,)),
            dma((2,)),
            dma((4,)),
            dma((REQS,)),
            dma((2 * MOVES,)),
            dma,
        ],
        compiler_params=params,
        name="front",
    )(
        *facts,
        frequency,
        tokens_now[0],
        tokens_next[0],
        norm_gain[None, :],
        key_weight,
        value_weight,
        query_weight,
        stored,
    )

    def send(size, bit, upward, parcel):
        moved = lax.ppermute(parcel[: size * STRIDE], "inst", route(bit, upward))
        return jnp.pad(moved, ((0, PARCEL - size * STRIDE), (0, 0)))

    sends = [
        functools.partial(send, size, bit, upward)
        for size in range(1, SIZES + 1)
        for bit in range(5)
        for upward in (0, 1)
    ]
    moved = lax.switch(way[0], sends, parcel)
    width = d // 4
    side = 2 * width + width // 4
    count = len(SPLITS)
    outs = (shape((REQS, d), BF16), shape((REQS + MOVES, d), BF16))
    raw = pl.pallas_call(
        out_kernel,
        out_shape=outs,
        in_specs=[hbm] * 3,
        out_specs=(vmem, vmem),
        scratch_shapes=[
            pltpu.VMEM(carried, F32),
            pltpu.VMEM((4, wide, width), BF16),
            pltpu.VMEM((PARCEL, 2 * HD), BF16),
            pltpu.VMEM((4, REQS, side), F32),
            pltpu.VMEM((3, REQS, side), F32),
            pltpu.VMEM((REQS, side), F32),
            pltpu.VMEM((REQS, side), F32),
            pltpu.VMEM((4, REQS, side), BF16),
            dma((2,)),
            dma((4,)),
            dma((count, 3)),
            dma((count, 3)),
            dma((count,)),
            dma((count,)),
            dma((count, 3)),
            dma((count, 3)),
        ],
        compiler_params=pltpu.CompilerParams(
            vmem_limit_bytes=LIMIT, collective_id=0, has_side_effects=True
        ),
        name="project_out",
    )(carry, moved, out_weight)
    arrival = (MOVES, 2, SPAN, HD)
    first, second, arrived = pl.pallas_call(
        finish_kernel,
        out_shape=outs + (shape(arrival, BF16),),
        in_specs=[hbm] * 6,
        out_specs=(hbm,) * 3,
        scratch_shapes=fact_room
        + [pltpu.VMEM((PARCEL + SPAN, 2 * HD), BF16)]
        + [pltpu.VMEM(out.shape, BF16) for out in outs]
        + [pltpu.VMEM(arrival, BF16), dma((3,)), dma((3,)), dma((2,)), dma((MOVES,))],
        compiler_params=params,
        name="finish",
    )(*facts, moved, *raw)
    return first[None], second[None], arrived[None]


def solution(mesh):
    in_specs = (
        P("inst", None, None),
        P("inst", None, None),
        P(),
        P(None, "tp"),
        P(None, "tp"),
        P(None, "tp"),
        P("tp", None),
        P("inst", None, None, None, "tp"),
        P(),
        P(),
        P(),
    )
    out_specs = (P("inst", None, None), P("inst", None, None), P("inst", None, None, None, "tp"))
    return jax.shard_map(body, mesh=mesh, in_specs=in_specs, out_specs=out_specs, check_vma=False)
```

```python
import functools
import math

import jax
import jax.numpy as jnp
import numpy as np
from jax import lax
from jax.experimental import pallas as pl
from jax.experimental.pallas import tpu as pltpu
from jax.sharding import PartitionSpec as P

HD = 128
ROPE_THETA = 500000.0
NORM_EPSILON = 1e-05
MESH = pl.DeviceIdType.MESH
F32 = jnp.float32
BF16 = jnp.bfloat16
LIMIT = 60 * 1024 * 1024

ROWS = 48
REQS = 16
MOVES = 4
SPAN = 480
TILE = 16
PARCEL = MOVES * SPAN
SIZES = (480, 720, 960, 1200, 1440, PARCEL)
SPLITS = (1024, 2304)


def role(lengths, pairing):
    me = lax.axis_index("inst")
    partner = pairing[me]
    mine = lengths[0, me]
    theirs = lengths[0, partner]
    for slot in range(1, REQS):
        mine = mine + lengths[slot, me]
        theirs = theirs + lengths[slot, partner]
    sender = (mine > theirs) | ((mine == theirs) & (me < partner))
    return me, partner, sender


def load(copies):
    started = []
    for source, target, semaphore in copies:
        copy = pltpu.make_async_copy(source, target, semaphore)
        copy.start()
        started.append(copy)
    return started


def softmax_rows(scores):
    largest = jnp.max(scores, axis=-1, keepdims=True)
    raised = jnp.exp(scores - largest)
    return raised / jnp.sum(raised, axis=-1, keepdims=True)


def score_block(query, keys, limit):
    scores = lax.dot_general(
        query.astype(BF16), keys, (((1,), (1,)), ((), ())), preferred_element_type=F32
    ) * (1.0 / math.sqrt(HD))
    lane_at = lax.broadcasted_iota(jnp.int32, scores.shape, 1)
    return jnp.where(lane_at <= limit, scores, -jnp.inf)


def front_kernel(
    lengths_hbm,
    pairing_hbm,
    moving_hbm,
    frequency_hbm,
    tokens_now_hbm,
    tokens_next_hbm,
    norm_gain_hbm,
    key_weight,
    value_weight,
    query_weight,
    kv_cache,
    parcel_hbm,
    carry_hbm,
    way_out,
    lengths,
    pairing,
    moving,
    frequency,
    tokens_now,
    tokens_next,
    norm_gain,
    key_held,
    value_held,
    query_held,
    cache,
    normed,
    new_key,
    new_value,
    query,
    scores,
    carry,
    fact_sem,
    token_sem,
    weight_sem,
    query_sem,
    cache_sem,
    parcel_sem,
    carry_sem,
):
    facts = load(
        [
            (lengths_hbm, lengths, fact_sem.at[0]),
            (pairing_hbm, pairing, fact_sem.at[1]),
            (moving_hbm, moving, fact_sem.at[2]),
            (frequency_hbm, frequency, fact_sem.at[3]),
        ]
    )
    tokens = load(
        [
            (tokens_now_hbm, tokens_now, token_sem.at[0]),
            (tokens_next_hbm, tokens_next, token_sem.at[1]),
            (norm_gain_hbm, norm_gain, token_sem.at[2]),
        ]
    )
    weights = load(
        [
            (key_weight, key_held, weight_sem.at[0]),
            (value_weight, value_held, weight_sem.at[1]),
        ]
    )
    depth = query_held.shape[0] // 4
    queries = load(
        [
            (
                query_weight.at[pl.ds(depth * part, depth)],
                query_held.at[pl.ds(depth * part, depth)],
                query_sem.at[part],
            )
            for part in range(4)
        ]
    )
    for slot in range(REQS):
        cache[slot, 1] = jnp.zeros((SPAN, HD), BF16)
    for copy in facts:
        copy.wait()
    me, partner, sender = role(lengths, pairing)
    caches = []
    for slot in range(REQS):
        size = pl.multiple_of(((lengths[slot, me] + 1) // TILE + 1) * TILE, TILE)
        caches.append(
            (
                kv_cache.at[slot, :, pl.ds(0, size)],
                cache.at[slot, :, pl.ds(0, size)],
                cache_sem.at[slot],
            )
        )
    caches = load(caches)
    total = 0
    giver = jnp.where(sender, me, partner)
    for move in range(MOVES):
        total = total + (lengths[moving[move, giver], giver] // TILE + 1) * TILE
    distance = me ^ partner
    bit = (
        (distance >= 2).astype(jnp.int32)
        + (distance >= 4).astype(jnp.int32)
        + (distance >= 8).astype(jnp.int32)
        + (distance >= 16).astype(jnp.int32)
    )
    upward = (sender == (me < partner)).astype(jnp.int32)
    size_class = 0
    for size in SIZES[:-1]:
        size_class = size_class + (total > size).astype(jnp.int32)
    way_out[0] = (size_class * 5 + bit) * 2 + upward

    row_at = lax.broadcasted_iota(jnp.int32, (ROWS, HD), 0)
    times = jnp.zeros((ROWS, HD), jnp.int32)
    for slot in range(REQS):
        times = jnp.where(row_at == slot, lengths[slot, me], times)
        times = jnp.where(row_at == REQS + slot, lengths[slot, me] + 1, times)
    for move in range(MOVES):
        in_length = lengths[moving[move, partner], partner]
        times = jnp.where(row_at == 2 * REQS + move, in_length + 1, times)
    angles = times.astype(F32) * frequency[...]
    lane_at = lax.broadcasted_iota(jnp.int32, (ROWS, HD), 1)
    cosine = jnp.cos(angles)
    sine = jnp.sin(angles)
    sine = jnp.where(lane_at < HD // 2, -sine, sine)

    for copy in tokens:
        copy.wait()
    gain = norm_gain[...]
    normed[2 * REQS :, :] = jnp.zeros((ROWS - 2 * REQS, normed.shape[1]), BF16)
    for rows, base in ((tokens_now, 0), (tokens_next, REQS)):
        count = rows.shape[0]
        widened = rows[...].astype(F32)
        scale = lax.rsqrt(jnp.mean(widened * widened, axis=-1, keepdims=True) + NORM_EPSILON)
        normed[base : base + count, :] = (widened * scale * gain).astype(BF16)

    for copy in weights:
        copy.wait()
    key = jnp.dot(normed[...], key_held[...], preferred_element_type=F32)
    value = jnp.dot(normed[...], value_held[...], preferred_element_type=F32)
    key = key * cosine + pltpu.roll(key, HD // 2, 1) * sine
    new_key[...] = key.astype(BF16).astype(F32)
    new_value[...] = value.astype(BF16).astype(F32)

    wide = query_held.shape[1]
    total = jnp.zeros((ROWS, wide), F32)
    for part in range(4):
        queries[part].wait()
        columns = slice(depth * part, depth * (part + 1))
        total = total + jnp.dot(
            normed[:, columns], query_held[columns, :], preferred_element_type=F32
        )
    carry[...] = jnp.zeros(carry.shape, F32)
    for head in range(4):
        columns = slice(head * HD, (head + 1) * HD)
        part = total[:, columns]
        part = part * cosine + pltpu.roll(part, HD // 2, 1) * sine
        part = part.astype(BF16).astype(F32)
        for slot in range(REQS):
            query[8 * slot + head : 8 * slot + head + 1, :] = part[slot : slot + 1]
            query[8 * slot + 4 + head : 8 * slot + 5 + head, :] = part[REQS + slot : REQS + slot + 1]
        for move in range(MOVES):
            at = ROWS + 4 * move + head
            carry[at : at + 1, :HD] = part[2 * REQS + move : 2 * REQS + move + 1]
    for slot in range(REQS):
        caches[slot].wait()
    window_at = lax.broadcasted_iota(jnp.int32, (2 * TILE, HD), 0)
    for group in range(0, REQS, 4):
        changed = []
        for slot in range(group, group + 4):
            length = lengths[slot, me]
            base = pl.multiple_of(jnp.minimum(length // TILE * TILE, SPAN - 2 * TILE), TILE)
            for kind, fresh in ((0, new_key), (1, new_value)):
                at = (slot, kind, pl.ds(base, 2 * TILE), slice(None))
                held = cache[at].astype(F32)
                for row, place in ((slot, length), (REQS + slot, length + 1)):
                    held = jnp.where(
                        window_at == place - base,
                        jnp.broadcast_to(fresh[row : row + 1, :], held.shape),
                        held,
                    )
                changed.append((at, held.astype(BF16)))
        for at, held in changed:
            cache[at] = held
    offset = 0
    parcels = []
    for move in range(MOVES):
        slot = moving[move, me]
        size = pl.multiple_of((lengths[slot, me] // TILE + 1) * TILE, TILE)
        start = pl.multiple_of(offset, TILE)
        for kind in range(2):
            parcels.append(
                (
                    cache.at[slot, kind, pl.ds(0, size)],
                    parcel_hbm.at[pl.ds(start, size), HD * kind : HD * (kind + 1)],
                    parcel_sem.at[2 * move + kind],
                )
            )
        offset = offset + size
    parcels = load(parcels)

    spot = lax.broadcasted_iota(jnp.int32, (4, HD), 1)
    receives = jnp.logical_not(sender).astype(jnp.int32)
    first = 0
    for move in range(MOVES):
        rows = slice(ROWS + 4 * move, ROWS + 4 * move + 4)
        own = slice(2 * REQS + move, 2 * REQS + move + 1)
        carry[rows, HD : 2 * HD] = jnp.broadcast_to(new_key[own, :], (4, HD))
        carry[rows, 2 * HD : 3 * HD] = jnp.broadcast_to(new_value[own, :], (4, HD))
        end = lengths[moving[move, partner], partner]
        marks = jnp.where(spot == 0, first, jnp.where(spot == 1, first + end, receives))
        carry[rows, 3 * HD :] = marks.astype(F32)
        first = first + (end // TILE + 1) * TILE
    late = (lax.broadcasted_iota(jnp.int32, (8, SPAN), 0) >= 4).astype(jnp.int32)
    for slot in range(REQS):
        scores[8 * slot : 8 * slot + 8, :] = score_block(
            query[8 * slot : 8 * slot + 8, :], cache[slot, 0], lengths[slot, me] + late
        )
    for group in range(4):
        rows = slice(32 * group, 32 * group + 32)
        scores[rows, :] = softmax_rows(scores[rows, :])
    for slot in range(REQS):
        mixed = jnp.dot(
            scores[8 * slot : 8 * slot + 8, :].astype(BF16),
            cache[slot, 1],
            preferred_element_type=F32,
        )
        for head in range(4):
            columns = slice(head * HD, (head + 1) * HD)
            carry[slot : slot + 1, columns] = mixed[head : head + 1]
            carry[REQS + slot : REQS + slot + 1, columns] = mixed[4 + head : 5 + head]
    row_at = lax.broadcasted_iota(jnp.int32, (REQS, wide), 0)
    gone = row_at < 0
    for move in range(MOVES):
        gone = gone | (row_at == moving[move, me])
    dead = gone & (jnp.broadcast_to(sender.astype(jnp.int32), gone.shape) == 1)
    carry[REQS : 2 * REQS, :] = jnp.where(dead, 0.0, carry[REQS : 2 * REQS, :])
    for copy in load([(carry, carry_hbm, carry_sem)]) + parcels:
        copy.wait()


def out_kernel(
    carry_hbm,
    parcel_hbm,
    out_weight,
    first_out,
    second_out,
    carry,
    weight_held,
    parcel,
    part,
    from_x,
    total,
    from_z,
    whole,
    fact_sem,
    weight_sem,
    x_send,
    x_recv,
    z_send,
    z_recv,
    g_send,
    g_recv,
):
    inst = lax.axis_index("inst")
    lane = lax.axis_index("tp")
    x = lane // 2
    z = lane % 2
    x_peers = [(inst, lax.rem(x + step, 4) * 2 + z) for step in range(1, 4)]
    z_peer = (inst, x * 2 + 1 - z)
    barrier = pltpu.get_barrier_semaphore()
    for peer in [z_peer] + x_peers:
        pl.semaphore_signal(barrier, inc=1, device_id=peer, device_id_type=MESH)
    width = weight_held.shape[2]
    quarter = width // 4
    order = (2, 1, 3, 0)
    facts = load([(carry_hbm, carry, fact_sem.at[0]), (parcel_hbm, parcel, fact_sem.at[1])])
    weights = load(
        [
            (
                out_weight.at[:, pl.ds(pl.multiple_of(lax.rem(x + step, 4) * width, width), width)],
                weight_held.at[step],
                weight_sem.at[step],
            )
            for step in order
        ]
    )

    facts[0].wait()
    rows = carry[:REQS, :].astype(BF16)
    for turn, step in enumerate(order):
        weights[turn].wait()
        part[step, :, :width] = jnp.dot(rows, weight_held[step], preferred_element_type=F32)
    edges = (0,) + SPLITS
    pieces = [slice(low, high) for low, high in zip(edges[:-1], edges[1:])]
    x_copies = {}
    z_copies = []
    g_copies = []
    def scatter(index):
        for step in order[:3]:
            copy = pltpu.make_async_remote_copy(
                src_ref=part.at[step, :, pieces[index]],
                dst_ref=from_x.at[step - 1, :, pieces[index]],
                send_sem=x_send.at[index, step - 1],
                recv_sem=x_recv.at[index, step - 1],
                device_id=x_peers[step - 1],
                device_id_type=MESH,
            )
            copy.start()
            x_copies[index, step] = copy

    pl.semaphore_wait(barrier, 4)
    scatter(0)

    facts[1].wait()
    query = carry[ROWS:, :HD]
    own_value = carry[ROWS:, 2 * HD : 3 * HD]
    scores = lax.dot_general(
        query.astype(BF16),
        parcel[:, :HD],
        (((1,), (1,)), ((), ())),
        preferred_element_type=F32,
    ) * (1.0 / math.sqrt(HD))
    lane_at = lax.broadcasted_iota(jnp.int32, scores.shape, 1).astype(F32)
    begin = jnp.broadcast_to(carry[ROWS:, 3 * HD : 3 * HD + 1], scores.shape)
    end = jnp.broadcast_to(carry[ROWS:, 3 * HD + 1 : 3 * HD + 2], scores.shape)
    scores = jnp.where((lane_at >= begin) & (lane_at <= end), scores, -jnp.inf)
    own_score = jnp.sum(query * carry[ROWS:, HD : 2 * HD], axis=-1, keepdims=True) * (
        1.0 / math.sqrt(HD)
    )
    largest = jnp.maximum(jnp.max(scores, axis=-1, keepdims=True), own_score)
    raised = jnp.exp(scores - largest)
    own_raised = jnp.exp(own_score - largest)
    below = jnp.sum(raised, axis=-1, keepdims=True) + own_raised
    own_weight = (own_raised / below).astype(BF16).astype(F32)
    mixed = jnp.dot(
        (raised / below).astype(BF16), parcel[:, HD:], preferred_element_type=F32
    ) + own_weight * own_value
    receives = jnp.broadcast_to(carry[ROWS:, 3 * HD + 2 : 3 * HD + 3], mixed.shape)
    mixed = jnp.where(receives > 0.5, mixed, 0.0)
    for move in range(MOVES):
        for head in range(4):
            at = 4 * move + head
            carry[2 * REQS + move : 2 * REQS + move + 1, HD * head : HD * (head + 1)] = mixed[
                at : at + 1
            ]

    rows = carry[REQS:ROWS, :].astype(BF16)
    for step in order:
        block = jnp.dot(rows, weight_held[step], preferred_element_type=F32)
        part[step, :, width : 2 * width] = block[:REQS]
        for at in range(4):
            part[step, 4 * at : 4 * at + 4, 2 * width :] = block[
                REQS : REQS + MOVES, quarter * at : quarter * (at + 1)
            ]
    scatter(1)
    for index, columns in enumerate(pieces):
        for step in order[:3]:
            x_copies[index, step].wait_recv()
        total[:, columns] = (part[0, :, columns] + from_x[0, :, columns]) + (
            from_x[1, :, columns] + from_x[2, :, columns]
        )
        copy = pltpu.make_async_remote_copy(
            src_ref=total.at[:, columns],
            dst_ref=from_z.at[:, columns],
            send_sem=z_send.at[index],
            recv_sem=z_recv.at[index],
            device_id=z_peer,
            device_id_type=MESH,
        )
        copy.start()
        z_copies.append(copy)
    for index, columns in enumerate(pieces):
        z_copies[index].wait_recv()
        whole[x, :, columns] = (total[:, columns] + from_z[:, columns]).astype(BF16)
        for step in order[:3]:
            copy = pltpu.make_async_remote_copy(
                src_ref=whole.at[x, :, columns],
                dst_ref=whole.at[x, :, columns],
                send_sem=g_send.at[index, step - 1],
                recv_sem=g_recv.at[index, step - 1],
                device_id=x_peers[step - 1],
                device_id_type=MESH,
            )
            copy.start()
            g_copies.append(copy)
    for copy in g_copies:
        copy.wait_recv()
    for chunk in range(4):
        columns = slice(chunk * width, (chunk + 1) * width)
        first_out[:, columns] = whole[chunk, :, :width]
        second_out[:REQS, columns] = whole[chunk, :, width : 2 * width]
        folded = whole[chunk, :, 2 * width :].astype(F32)
        spread = [folded[4 * at : 4 * at + 4] for at in range(4)]
        second_out[REQS:, columns] = jnp.concatenate(spread, axis=1).astype(BF16)
    for copy in list(x_copies.values()) + z_copies + g_copies:
        copy.wait_send()


def finish_kernel(
    lengths_hbm,
    pairing_hbm,
    moving_hbm,
    parcel_hbm,
    first_in,
    second_in,
    first_out,
    second_out,
    arrived_out,
    lengths,
    pairing,
    moving,
    parcel,
    first,
    second,
    arrived,
    fact_sem,
    in_sem,
    out_sem,
    arrived_sem,
):
    facts = load(
        [
            (lengths_hbm, lengths, fact_sem.at[0]),
            (pairing_hbm, pairing, fact_sem.at[1]),
            (moving_hbm, moving, fact_sem.at[2]),
        ]
    )
    reads = load(
        [
            (parcel_hbm, parcel.at[pl.ds(0, PARCEL)], in_sem.at[0]),
            (first_in, first, in_sem.at[1]),
            (second_in, second, in_sem.at[2]),
        ]
    )
    for copy in facts:
        copy.wait()
    me, partner, sender = role(lengths, pairing)
    reads[0].wait()
    row_at = lax.broadcasted_iota(jnp.int32, (SPAN, HD), 0)
    offset = 0
    writes = []
    for move in range(MOVES):
        end = lengths[moving[move, partner], partner]
        last = jnp.where(sender, -1, end)
        start = pl.multiple_of(offset, TILE)
        for kind in range(2):
            block = parcel[pl.ds(start, SPAN), HD * kind : HD * (kind + 1)].astype(F32)
            arrived[move, kind] = jnp.where(row_at <= last, block, 0.0).astype(BF16)
        offset = offset + (end // TILE + 1) * TILE
        writes += load([(arrived.at[move], arrived_out.at[move], arrived_sem.at[move])])
    for index, pair in enumerate(((first, first_out), (second, second_out))):
        reads[index + 1].wait()
        writes += load([pair + (out_sem.at[index],)])
    for copy in writes:
        copy.wait()


def route(bit, upward):
    pairs = []
    for low in range(32):
        high = low | 1 << bit
        if high != low:
            pairs.append((low, high) if upward else (high, low))
    return pairs


def body(
    tokens_now,
    tokens_next,
    norm_gain,
    query_weight,
    key_weight,
    value_weight,
    out_weight,
    kv_cache,
    lengths,
    pairing,
    moving,
):
    vmem = pl.BlockSpec(memory_space=pltpu.VMEM)
    smem = pl.BlockSpec(memory_space=pltpu.SMEM)
    hbm = pl.BlockSpec(memory_space=pl.ANY)
    params = pltpu.CompilerParams(vmem_limit_bytes=LIMIT)
    d = tokens_now.shape[-1]
    wide = query_weight.shape[1]
    stored = kv_cache[0]
    half = ROPE_THETA ** (-(np.arange(HD // 2, dtype=np.float32) * 2.0) / HD)
    frequency = np.concatenate([half, half]).astype(np.float32)[None, :]
    shape = jax.ShapeDtypeStruct
    dma = pltpu.SemaphoreType.DMA
    facts = (lengths.T, pairing, moving.T)
    fact_room = [pltpu.SMEM(fact.shape, jnp.int32) for fact in facts]
    carried = (ROWS + 16, wide)
    parcel, carry, way = pl.pallas_call(
        front_kernel,
        out_shape=(
            shape((PARCEL, 2 * HD), BF16),
            shape(carried, F32),
            shape((1,), jnp.int32),
        ),
        in_specs=[hbm] * 11,
        out_specs=(hbm, hbm, smem),
        scratch_shapes=fact_room
        + [
            pltpu.VMEM((1, HD), F32),
            pltpu.VMEM((REQS, d), BF16),
            pltpu.VMEM((REQS + MOVES, d), BF16),
            pltpu.VMEM((1, d), F32),
            pltpu.VMEM((d, HD), BF16),
            pltpu.VMEM((d, HD), BF16),
            pltpu.VMEM((d, wide), BF16),
            pltpu.VMEM(stored.shape, BF16),
            pltpu.VMEM((ROWS, d), BF16),
            pltpu.VMEM((ROWS, HD), F32),
            pltpu.VMEM((ROWS, HD), F32),
            pltpu.VMEM((8 * REQS, HD), F32),
            pltpu.VMEM((8 * REQS, SPAN), F32),
            pltpu.VMEM(carried, F32),
            dma((4,)),
            dma((3,)),
            dma((2,)),
            dma((4,)),
            dma((REQS,)),
            dma((2 * MOVES,)),
            dma,
        ],
        compiler_params=params,
        name="front",
    )(
        *facts,
        frequency,
        tokens_now[0],
        tokens_next[0],
        norm_gain[None, :],
        key_weight,
        value_weight,
        query_weight,
        stored,
    )

    def send(size, bit, upward, parcel):
        moved = lax.ppermute(parcel[:size], "inst", route(bit, upward))
        return jnp.pad(moved, ((0, PARCEL - size), (0, 0)))

    sends = [
        functools.partial(send, size, bit, upward)
        for size in SIZES
        for bit in range(5)
        for upward in (0, 1)
    ]
    moved = lax.switch(way[0], sends, parcel)
    width = d // 4
    side = 2 * width + width // 4
    count = len(SPLITS)
    outs = (shape((REQS, d), BF16), shape((REQS + MOVES, d), BF16))
    raw = pl.pallas_call(
        out_kernel,
        out_shape=outs,
        in_specs=[hbm] * 3,
        out_specs=(vmem, vmem),
        scratch_shapes=[
            pltpu.VMEM(carried, F32),
            pltpu.VMEM((4, wide, width), BF16),
            pltpu.VMEM((PARCEL, 2 * HD), BF16),
            pltpu.VMEM((4, REQS, side), F32),
            pltpu.VMEM((3, REQS, side), F32),
            pltpu.VMEM((REQS, side), F32),
            pltpu.VMEM((REQS, side), F32),
            pltpu.VMEM((4, REQS, side), BF16),
            dma((2,)),
            dma((4,)),
            dma((count, 3)),
            dma((count, 3)),
            dma((count,)),
            dma((count,)),
            dma((count, 3)),
            dma((count, 3)),
        ],
        compiler_params=pltpu.CompilerParams(
            vmem_limit_bytes=LIMIT, collective_id=0, has_side_effects=True
        ),
        name="project_out",
    )(carry, moved, out_weight)
    arrival = (MOVES, 2, SPAN, HD)
    first, second, arrived = pl.pallas_call(
        finish_kernel,
        out_shape=outs + (shape(arrival, BF16),),
        in_specs=[hbm] * 6,
        out_specs=(hbm,) * 3,
        scratch_shapes=fact_room
        + [pltpu.VMEM((PARCEL + SPAN, 2 * HD), BF16)]
        + [pltpu.VMEM(out.shape, BF16) for out in outs]
        + [pltpu.VMEM(arrival, BF16), dma((3,)), dma((3,)), dma((2,)), dma((MOVES,))],
        compiler_params=params,
        name="finish",
    )(*facts, moved, *raw)
    return first[None], second[None], arrived[None]


def solution(mesh):
    in_specs = (
        P("inst", None, None),
        P("inst", None, None),
        P(),
        P(None, "tp"),
        P(None, "tp"),
        P(None, "tp"),
        P("tp", None),
        P("inst", None, None, None, "tp"),
        P(),
        P(),
        P(),
    )
    out_specs = (P("inst", None, None), P("inst", None, None), P("inst", None, None, None, "tp"))
    return jax.shard_map(body, mesh=mesh, in_specs=in_specs, out_specs=out_specs, check_vma=False)
```
